768 devices in a mesh: ctx: 32 (over y, z_lo), head: 24 (over z_hi, x, core).
Axes of the slice: x: 4, y: 8, z: 12 (z_hi: 3, z_lo: 4; z = z_hi * 4 + z_lo), core: 2. Of those that a mesh axis runs over, the one named last changes fastest.
Arguments:
- queries: bfloat16 [16384, 96, 128], P('ctx', 'head'), may hold values from -16 to 16
- keys: bfloat16 [16384, 6, 128], P('ctx'), may hold values from -6 to 6
- values: bfloat16 [16384, 6, 128], P('ctx'), may hold values from -6 to 6
- d_out: bfloat16 [16384, 96, 128], P('ctx', 'head'), may hold values from -1.796875 to 1.796875
- block_pos: int32 [4, 32], replicated, may hold values from 0 to 31, each once within a row
- block_mask: int32 [4, 32, 32], replicated, may hold values 0 or 1
Outputs:
- d_queries: bfloat16 [16384, 96, 128], P('ctx', 'head')
- d_keys: bfloat16 [16384, 6, 128], P('ctx')
- d_values: bfloat16 [16384, 6, 128], P('ctx')
The draws below stay inside these ranges and needn't reach their ends.
Inputs may be any that keep to these rules, and one draw needn't show every extreme that they name: `block_pos`: each row holds each of the 32 block numbers once. `block_mask`: only entries [s, i, i2] with i2 < i are read.
All inputs are finite; a program needn't handle non-finite values.
Results may differ from the reference program's by a relative error of at most 0.0075.
Values may be sent and summed in bfloat16 or wider, within the bound.
A program may use at most 32 MiB of HBM per device.

```python
import jax
import jax.numpy as jnp
from jax import lax

HD = 128
GROUP = 16
BLK = 128
SEQS = 4
QB_DEV = 4
HQ = 96
KVH = 6
TOKENS = 16384
LEN = 4096
NBLK = 32
N_CTX = 32


def query_key_pair(key):
    base = jax.random.fold_in(key, 7101)
    first, second = jax.random.split(base, 2)
    query_draw = jnp.clip(jax.random.normal(first, (TOKENS, HQ, HD), jnp.float32), -4.5, 4.5)
    key_draw = jnp.clip(jax.random.normal(second, (TOKENS, KVH, HD), jnp.float32), -4.5, 4.5)
    return (query_draw, key_draw)


def draw_queries(key, part):
    return query_key_pair(key)[0].astype(jnp.bfloat16)


def draw_keys(key, part):
    return query_key_pair(key)[1].astype(jnp.bfloat16)


def with_ends(values, key, low, top_value):
    index_at = [jax.random.randint(jax.random.fold_in(key, axis), (), 0, length) for axis, length in enumerate(values.shape)]
    longest = values.shape.index(max(values.shape))
    beside = index_at[:longest] + [(index_at[longest] + 1) % values.shape[longest]] + index_at[longest + 1:]
    return values.at[tuple(index_at)].set(low).at[tuple(beside)].set(top_value)


def block_levels(key, dims, shards, least, high):
    def one(position, blocks):
        draws = jax.random.uniform(jax.random.fold_in(jax.random.fold_in(key, 6), position), (blocks,), jnp.float32, least / len(shards), high / len(shards))
        return jnp.repeat(jnp.exp(draws), dims[position] // blocks).reshape((-1,) + (1,) * (len(dims) - position - 1))

    gain = one(*shards[0])
    for cut in shards[1:]:
        gain = gain * one(*cut)
    return gain


def gaussian(rng, shape, spread, most, cuts=(), kind=jnp.bfloat16):
    values = spread * jax.random.normal(rng, shape, jnp.float32)
    if cuts:
        values = values * block_levels(rng, shape, cuts, -0.22, 0.18)
    return jnp.clip(values, -most, most).astype(kind)


def setup_inputs(seed: int = 0) -> dict:
    key_of = jax.random.split(jax.random.key(seed), 7)
    return {
        "queries": draw_queries(jax.random.fold_in(key_of[6], 71), 0),
        "keys": draw_keys(jax.random.fold_in(key_of[6], 71), 0),
        "values": gaussian(key_of[2], (TOKENS, KVH, HD), 1.0, 6.0, ((0, 32),)),
        "d_out": gaussian(key_of[3], (TOKENS, HQ, HD), 0.3, 1.796875, ((0, 32), (1, 24))),
        "block_pos": jax.vmap(lambda own: jax.random.permutation(own, NBLK))(jax.random.split(key_of[4], SEQS)).reshape((SEQS, NBLK)).astype(jnp.int32),
        "block_mask": with_ends((jax.random.randint(key_of[5], (SEQS, NBLK, NBLK), 0, 2) < 1).astype(jnp.int32), jax.random.fold_in(key_of[5], 1), 0, 1),
    }


def contract_rows(left, right):
    return jnp.dot(left, right.T, preferred_element_type=jnp.float32)


def to_sequences(stored, members):
    width = stored.shape[1]
    depth = stored.shape[2]
    grouped = stored.reshape(members, SEQS, QB_DEV * BLK, width, depth)
    return jnp.transpose(grouped, (1, 0, 2, 3, 4)).reshape(SEQS, LEN, width, depth)


def to_stored(ordered, members):
    width = ordered.shape[2]
    depth = ordered.shape[3]
    grouped = ordered.reshape(SEQS, members, QB_DEV * BLK, width, depth)
    return jnp.transpose(grouped, (1, 0, 2, 3, 4)).reshape(TOKENS, width, depth)


def reference(queries, keys, values, d_out, block_pos, block_mask):
    members = N_CTX // SEQS
    score_scale = HD ** -0.5
    block_rows = BLK * GROUP

    def head_groups(stored):
        ordered = to_sequences(stored, members).reshape(SEQS, LEN, KVH, GROUP, HD)
        return jnp.transpose(ordered, (0, 2, 1, 3, 4)).reshape(SEQS * KVH, LEN * GROUP, HD)

    def kv_groups(stored):
        ordered = to_sequences(stored, members)
        return jnp.transpose(ordered, (0, 2, 1, 3)).reshape(SEQS * KVH, LEN, HD)

    operands = (head_groups(queries), head_groups(d_out), kv_groups(keys), kv_groups(values),
                jnp.repeat(block_pos, KVH, axis=0), jnp.repeat(block_mask, KVH, axis=0))

    def one_group(group_operands):
        query_rows, grad_rows, key_rows, value_rows, order, mask_table = group_operands

        def visible(query_slot, key_slot):
            query_block = order[query_slot]
            key_block = order[key_slot]
            earlier = jnp.logical_and(key_block < query_block, mask_table[query_block, key_block] == 1)
            return jnp.logical_or(query_slot == key_slot, earlier)

        def row_slice(array, slot, count):
            return lax.dynamic_slice_in_dim(array, (slot * count).astype(jnp.int32), count, 0)

        def logits_of(query_slot, key_slot):
            q_block = row_slice(query_rows, query_slot, block_rows)
            k_block = row_slice(key_rows, key_slot, BLK)
            logits = contract_rows(q_block, k_block) * score_scale
            query_token = lax.broadcasted_iota(jnp.int32, logits.shape, 0) // GROUP
            key_token = lax.broadcasted_iota(jnp.int32, logits.shape, 1)
            allowed = jnp.logical_or(query_slot != key_slot, key_token <= query_token)
            return jnp.where(allowed, logits, -jnp.inf)

        def stats_block(query_slot):
            g_block = row_slice(grad_rows, query_slot, block_rows)

            def visit(key_slot, running):
                def update(running):
                    maxima, totals, weighted = running
                    logits = logits_of(query_slot, key_slot)
                    v_block = row_slice(value_rows, key_slot, BLK)
                    dprob_rows = contract_rows(g_block, v_block)
                    new_max = jnp.maximum(maxima, jnp.max(logits, axis=1))
                    factor = jnp.exp(maxima - new_max)
                    exp_rows = jnp.exp(logits - new_max[:, None])
                    return (new_max, totals * factor + jnp.sum(exp_rows, axis=1),
                            weighted * factor + jnp.sum(exp_rows * dprob_rows, axis=1))
                return lax.cond(visible(query_slot, key_slot), update, lambda kept: kept, running)

            initial = (jnp.full((block_rows,), -jnp.inf, jnp.float32), jnp.zeros((block_rows,), jnp.float32),
                       jnp.zeros((block_rows,), jnp.float32))
            maxima, totals, weighted = lax.fori_loop(0, NBLK, visit, initial)
            return maxima + jnp.log(totals), weighted / totals

        log_sums, deltas = lax.map(stats_block, jnp.arange(NBLK, dtype=jnp.int32))

        def grad_block(key_sums, query_slot):
            q_block = row_slice(query_rows, query_slot, block_rows)
            g_block = row_slice(grad_rows, query_slot, block_rows)
            log_row = log_sums[query_slot]
            delta_row = deltas[query_slot]

            def visit(key_slot, running):
                def update(running):
                    query_grad, key_sums = running
                    logits = logits_of(query_slot, key_slot)
                    k_block = row_slice(key_rows, key_slot, BLK)
                    v_block = row_slice(value_rows, key_slot, BLK)
                    prob_rows = jnp.exp(logits - log_row[:, None])
                    dprob_rows = contract_rows(g_block, v_block)
                    dscore = (prob_rows * (dprob_rows - delta_row[:, None])).astype(jnp.bfloat16)
                    query_grad = query_grad + jnp.dot(dscore, k_block, preferred_element_type=jnp.float32)
                    key_add = jnp.dot(dscore.T, q_block, preferred_element_type=jnp.float32)
                    value_add = jnp.dot(prob_rows.astype(jnp.bfloat16).T, g_block, preferred_element_type=jnp.float32)
                    key_start = (key_slot * BLK).astype(jnp.int32)
                    previous = lax.dynamic_slice_in_dim(key_sums, key_start, BLK, 1)
                    key_sums = lax.dynamic_update_slice_in_dim(key_sums, previous + jnp.stack([key_add, value_add]), key_start, 1)
                    return query_grad, key_sums
                return lax.cond(visible(query_slot, key_slot), update, lambda kept: kept, running)

            query_grad, key_sums = lax.fori_loop(0, NBLK, visit, (jnp.zeros((block_rows, HD), jnp.float32), key_sums))
            return key_sums, query_grad

        key_sums, query_grads = lax.scan(grad_block, jnp.zeros((2, LEN, HD), jnp.float32), jnp.arange(NBLK, dtype=jnp.int32))
        d_query = (query_grads.reshape(LEN * GROUP, HD) * score_scale).astype(jnp.bfloat16)
        d_key = (key_sums[0] * score_scale).astype(jnp.bfloat16)
        d_value = key_sums[1].astype(jnp.bfloat16)
        return d_query, d_key, d_value

    query_out, key_out, value_out = lax.map(one_group, operands)
    query_seq = jnp.transpose(query_out.reshape(SEQS, KVH, LEN, GROUP, HD), (0, 2, 1, 3, 4)).reshape(SEQS, LEN, HQ, HD)
    key_seq = jnp.transpose(key_out.reshape(SEQS, KVH, LEN, HD), (0, 2, 1, 3))
    value_seq = jnp.transpose(value_out.reshape(SEQS, KVH, LEN, HD), (0, 2, 1, 3))
    return to_stored(query_seq, members), to_stored(key_seq, members), to_stored(value_seq, members)
```

```python
import functools
import math

import jax
import jax.numpy as jnp
from jax import lax
from jax.experimental import pallas as pl
from jax.experimental.pallas import tpu as pltpu
from jax.sharding import PartitionSpec as P

GROUP = 16
BLK = 128
SEQS = 4
QB_DEV = 4
CORES = 2
X = 4
NEG = -1e30
VMEM_BYTES = 60 * 1024 * 1024
MESH = pl.DeviceIdType.MESH


class Place:
    def __init__(self, members, planes):
        self.members = members
        self.planes = planes
        ctx = lax.axis_index("ctx")
        head = lax.axis_index("head")
        self.seq = ctx % SEQS
        self.y = ctx // SEQS
        self.core = head % CORES
        self.x = head // CORES % X
        self.z = head // (CORES * X)
        self.ctx = ctx
        self.head = head

    def member(self, steps):
        return (self.y + steps + self.members) % self.members

    def along_y(self, steps):
        return (self.member(steps) * SEQS + self.seq, self.head)

    def head_id(self, z, x, core):
        return (self.ctx, (z * X + x) * CORES + core)

    def sibling(self):
        return self.head_id(self.z, self.x, 1 - self.core)


def meet(partners):
    barrier = pltpu.get_barrier_semaphore()
    for partner in partners:
        pl.semaphore_signal(barrier, inc=1, device_id=partner, device_id_type=MESH)
    pl.semaphore_wait(barrier, len(partners))


def remote(src, dst, send_sem, recv_sem, target):
    return pltpu.make_async_remote_copy(
        src_ref=src,
        dst_ref=dst,
        send_sem=send_sem,
        recv_sem=recv_sem,
        device_id=target,
        device_id_type=MESH,
    )


def gather_kernel(members, planes, kv_per_plane, k_ref, v_ref, kg_ref, vg_ref, own_sem,
                  send_sem, recv_sem, side_send, side_recv):
    place = Place(members, planes)
    half_way = members // 2
    rows = k_ref.shape[1]
    part = rows // CORES
    kv = place.z * kv_per_plane + place.x * kv_per_plane // X
    mine = pl.ds(place.core * part, part)
    other = pl.ds((1 - place.core) * part, part)
    pairs = ((k_ref, kg_ref), (v_ref, vg_ref))
    own = [
        pltpu.make_async_copy(src.at[kv], dst.at[place.y], own_sem.at[index])
        for index, (src, dst) in enumerate(pairs)
    ]
    meet([place.along_y(1), place.along_y(-1), place.sibling()])
    started = []
    chains = []
    for tensor in range(2):
        for way, sign in enumerate((1, -1)):
            hops = half_way if tensor == way else half_way - 1
            chains.append((tensor, way, sign, hops))

    def ring_copy(tensor, way, sign, step):
        src_in, dst = pairs[tensor]
        at = dst.at[place.member(-sign * step), mine]
        src = src_in.at[kv, mine] if step == 0 else at
        return remote(
            src, at, send_sem.at[tensor, way, step], recv_sem.at[tensor, way, step], place.along_y(sign)
        )

    def arrival(tensor, way, sign, step):
        at = pairs[tensor][1].at[place.member(-sign * (step + 1)), mine]
        return remote(
            at, at, send_sem.at[tensor, way, step], recv_sem.at[tensor, way, step], place.along_y(sign)
        )

    def side_copy(tensor, way, sign, step, rows_at):
        at = pairs[tensor][1].at[place.member(-sign * (step + 1)), rows_at]
        return remote(
            at, at, side_send.at[tensor, way, step], side_recv.at[tensor, way, step], place.sibling()
        )

    for chain in chains:
        copy = ring_copy(*chain[:3], 0)
        copy.start()
        started.append(copy)
    for copy in own:
        copy.start()
    for step in range(half_way):
        for tensor, way, sign, hops in chains:
            if step >= hops:
                continue
            arrival(tensor, way, sign, step).wait_recv()
            if step + 1 < hops:
                copy = ring_copy(tensor, way, sign, step + 1)
                copy.start()
                started.append(copy)
            copy = side_copy(tensor, way, sign, step, mine)
            copy.start()
            started.append(copy)
    for tensor, way, sign, hops in chains:
        for step in range(hops):
            side_copy(tensor, way, sign, step, other).wait_recv()
    for copy in started:
        copy.wait_send()
    for copy in own:
        copy.wait()


def gather(members, planes, keys, values):
    kv_count, rows, depth = keys.shape
    out = jax.ShapeDtypeStruct((members, rows, depth), keys.dtype)
    hops = members // 2
    return pl.pallas_call(
        functools.partial(gather_kernel, members, planes, kv_count // planes),
        out_shape=(out, out),
        in_specs=[pl.BlockSpec(memory_space=pl.ANY)] * 2,
        out_specs=[pl.BlockSpec(memory_space=pl.ANY)] * 2,
        scratch_shapes=[pltpu.SemaphoreType.DMA((2,))]
        + [pltpu.SemaphoreType.DMA((2, 2, hops))] * 4,
        compiler_params=pltpu.CompilerParams(collective_id=0, has_side_effects=True),
        name="gather_keys",
    )(keys, values)


def dot(left, right):
    return jnp.dot(left, right, preferred_element_type=jnp.float32)


def dot_first(left, right):
    return lax.dot_general(left, right, (((0,), (0,)), ((), ())), preferred_element_type=jnp.float32)


def grad_kernel(members, order_ref, mask_ref, q_ref, g_ref, k_ref, v_ref, dq_ref, dkv_ref,
                list_ref, score_ref, dprob_ref, acc_ref, dq_acc, qt_ref, gt_ref):
    ctx = lax.axis_index("ctx")
    seq = ctx % SEQS
    member = ctx // SEQS
    depth = q_ref.shape[1]
    rows = q_ref.shape[0] // QB_DEV
    heads = rows // BLK
    slots = members * QB_DEV
    scale = depth ** -0.5
    scale2 = scale * math.log2(math.e)
    acc_ref[...] = jnp.zeros_like(acc_ref)

    def pair(ref, first, second):
        return jnp.concatenate([ref[first], ref[second]], axis=0)

    def fold(value, op):
        return op(value.reshape(value.shape[0] // 8, 8, rows), axis=0)

    def spread(value, like):
        count = like.shape[0]
        return jnp.broadcast_to(value[None], (count // 8, 8, rows)).reshape(count, rows)

    def query_block(index, carry):
        own = member * QB_DEV + index
        query_pos = order_ref[seq, own]

        def list_slot(slot, count):
            key_pos = order_ref[seq, slot]
            list_ref[count] = slot
            seen = jnp.logical_and(key_pos < query_pos, mask_ref[seq, query_pos, key_pos] == 1)
            return count + seen.astype(jnp.int32)

        count = lax.fori_loop(0, slots, list_slot, 0, unroll=8)
        pairs = count // 2
        odd = count % 2 == 1
        at = pl.ds(pl.multiple_of(index * rows, rows), rows)
        qt_ref[...] = q_ref[at, :].T
        gt_ref[...] = g_ref[at, :].T

        def place_of(number):
            return pl.ds(pl.multiple_of(BLK + number * 2 * BLK, BLK), 2 * BLK)

        tail_at = pl.ds(pl.multiple_of(BLK + pairs * 2 * BLK, BLK), BLK)

        def over(diagonal, two, one, init):
            state = diagonal(init)

            def body(number, state):
                first, second = list_ref[2 * number], list_ref[2 * number + 1]
                return two(first, second, place_of(number), state)

            state = lax.fori_loop(0, pairs, body, state)
            return lax.cond(odd, lambda kept: one(list_ref[2 * pairs], tail_at, kept), lambda kept: kept, state)

        first_at = pl.ds(0, BLK)

        def score_diagonal(maxima):
            score = dot(k_ref[own], qt_ref[...])
            key_token = lax.broadcasted_iota(jnp.int32, (BLK, rows), 0)
            query_token = lax.broadcasted_iota(jnp.int32, (BLK, rows), 1) // heads
            score = jnp.where(key_token <= query_token, score, NEG)
            score_ref[first_at, :] = score
            return jnp.maximum(maxima, fold(score, jnp.max))

        def score_two(first, second, where, maxima):
            score = dot(pair(k_ref, first, second), qt_ref[...])
            score_ref[where, :] = score
            return jnp.maximum(maxima, fold(score, jnp.max))

        def score_one(slot, where, maxima):
            score = dot(k_ref[slot], qt_ref[...])
            score_ref[where, :] = score
            return jnp.maximum(maxima, fold(score, jnp.max))

        maxima = over(score_diagonal, score_two, score_one, jnp.full((8, rows), NEG, jnp.float32))
        top = jnp.broadcast_to(jnp.max(maxima, axis=0, keepdims=True), (8, rows)) * scale2

        def weigh(values, where, state):
            totals, weighted = state
            dprob = dot(values, gt_ref[...])
            score = score_ref[where, :]
            exp_part = jnp.exp2(score * scale2 - spread(top, score))
            score_ref[where, :] = exp_part
            dprob_ref[where, :] = dprob
            return totals + fold(exp_part, jnp.sum), weighted + fold(exp_part * dprob, jnp.sum)

        zero = jnp.zeros((8, rows), jnp.float32)
        totals, weighted = over(
            lambda state: weigh(v_ref[own], first_at, state),
            lambda first, second, where, state: weigh(pair(v_ref, first, second), where, state),
            lambda slot, where, state: weigh(v_ref[slot], where, state),
            (zero, zero),
        )
        total = jnp.sum(totals, axis=0, keepdims=True)
        inverse = 1.0 / total
        delta = jnp.broadcast_to(jnp.sum(weighted, axis=0, keepdims=True) * inverse, (8, rows))
        inverse = jnp.broadcast_to(inverse, (8, rows))

        def grads(where):
            exp_part = score_ref[where, :]
            prob = exp_part * spread(inverse, exp_part)
            dscore = prob * (dprob_ref[where, :] - spread(delta, exp_part))
            return prob.astype(jnp.bfloat16), dscore.astype(jnp.bfloat16)

        def grad_one(slot, where, first=False):
            prob, dscore = grads(where)
            acc_ref[0, slot] += dot(dscore, q_ref[at, :])
            acc_ref[1, slot] += dot(prob, g_ref[at, :])
            add = dot_first(dscore, k_ref[slot])
            dq_acc[...] = add if first else dq_acc[...] + add

        def grad_two(first, second, where):
            prob, dscore = grads(where)
            key_add = dot(dscore, q_ref[at, :])
            value_add = dot(prob, g_ref[at, :])
            acc_ref[0, first] += key_add[:BLK]
            acc_ref[0, second] += key_add[BLK:]
            acc_ref[1, first] += value_add[:BLK]
            acc_ref[1, second] += value_add[BLK:]
            dq_acc[...] += dot_first(dscore, pair(k_ref, first, second))

        grad_one(own, first_at, True)

        def grad_body(number, kept):
            grad_two(list_ref[2 * number], list_ref[2 * number + 1], place_of(number))
            return kept

        lax.fori_loop(0, pairs, grad_body, 0)

        @pl.when(odd)
        def _():
            grad_one(list_ref[2 * pairs], tail_at)

        dq_ref[at, :] = (dq_acc[...] * scale).astype(dq_ref.dtype)
        return carry

    lax.fori_loop(0, QB_DEV, query_block, 0)
    dkv_ref[0] = (acc_ref[0] * scale).astype(dkv_ref.dtype)
    dkv_ref[1] = acc_ref[1].astype(dkv_ref.dtype)


def local_grads(members, block_pos, block_mask, query_rows, grad_rows, keys, values):
    row_total, depth = query_rows.shape
    slots = members * QB_DEV
    rows = row_total // QB_DEV
    smem = pl.BlockSpec(memory_space=pltpu.SMEM)
    vmem = pl.BlockSpec(memory_space=pltpu.VMEM)
    return pl.pallas_call(
        functools.partial(grad_kernel, members),
        out_shape=(
            jax.ShapeDtypeStruct((row_total, depth), jnp.bfloat16),
            jax.ShapeDtypeStruct((2, slots, BLK, depth), jnp.bfloat16),
        ),
        in_specs=[smem, smem, vmem, vmem, vmem, vmem],
        out_specs=(vmem, vmem),
        scratch_shapes=[
            pltpu.SMEM((slots + 1,), jnp.int32),
            pltpu.VMEM(((slots + 2) * BLK, rows), jnp.float32),
            pltpu.VMEM(((slots + 2) * BLK, rows), jnp.float32),
            pltpu.VMEM((2, slots, BLK, depth), jnp.float32),
            pltpu.VMEM((rows, depth), jnp.float32),
            pltpu.VMEM((depth, rows), jnp.bfloat16),
            pltpu.VMEM((depth, rows), jnp.bfloat16),
        ],
        compiler_params=pltpu.CompilerParams(vmem_limit_bytes=VMEM_BYTES),
        name="local_grads",
    )(block_pos, block_mask, query_rows, grad_rows,
      keys.reshape(slots, BLK, depth), values.reshape(slots, BLK, depth))


def reduce_kernel(members, planes, part_ref, out_ref, side, sums, landed, total, piece, swap,
                  side_send, side_recv, ring_send, ring_recv, pair_sem, own_sem,
                  z_send, z_recv, x_send, x_recv, twin_send, twin_recv):
    place = Place(members, planes)
    half_way = members // 2
    rows = part_ref.shape[2]
    half = rows // 2
    core = place.core
    pair_x = place.x + 1 - 2 * (place.x % 2)
    partner = place.head_id(place.z, pair_x, core)
    z_ids = [(place.z + step) % planes for step in range(1, planes)]
    x_ids = [(place.x + step) % X for step in range(1, X)]
    meet(
        [place.along_y(1), place.along_y(-1), place.sibling()]
        + [place.head_id(place.z, x, core) for x in x_ids]
        + [place.head_id(z, place.x, core) for z in z_ids]
    )
    started = []

    def start(copy):
        copy.start()
        started.append(copy)

    offsets = [half_way]
    for steps in range(half_way - 1, 0, -1):
        offsets += [steps, -steps]
    offsets.append(0)

    def side_copy(steps):
        at = place.member(steps)
        slot = offsets.index(steps)
        return remote(part_ref.at[1 - core, at], side.at[slot], side_send.at[slot], side_recv.at[slot], place.sibling())

    for steps in offsets:
        start(side_copy(steps))

    def base(steps, which):
        slot = offsets.index(steps)
        at = place.member(steps)
        rows_at = pl.ds(which * half, half)
        return (part_ref[core, at, rows_at, :].astype(jnp.float32)
                + side[slot, rows_at, :].astype(jnp.float32))

    def ring_copy(way, step, which):
        return remote(
            sums.at[way, step, which],
            landed.at[way, step, which],
            ring_send.at[way, step, which],
            ring_recv.at[way, step, which],
            place.along_y(1 - 2 * way),
        )

    def begins(way, which):
        return 0 if way == which else 1

    def ring_step(way, step, which):
        sign = 1 - 2 * way
        steps = sign * (half_way - step)
        value = base(half_way if step == 0 else steps, which)
        if step > begins(way, which):
            ring_copy(way, step - 1, which).wait_recv()
            value = value + landed[way, step - 1, which].astype(jnp.float32)
        sums[way, step, which] = value.astype(sums.dtype)
        start(ring_copy(way, step, which))

    side_copy(half_way).wait_recv()
    ring_step(0, 0, 0)
    ring_step(1, 0, 1)
    for step in range(1, half_way):
        order = ((0, 1), (1, 0), (0, 0), (1, 1)) if step == 1 else ((0, 0), (1, 1), (0, 1), (1, 0))
        waited = set()
        for way, which in order:
            steps = (1 - 2 * way) * (half_way - step)
            if steps not in waited:
                side_copy(steps).wait_recv()
                waited.add(steps)
            ring_step(way, step, which)
    side_copy(0).wait_recv()
    for which in range(2):
        value = base(0, which)
        for way in range(2):
            ring_copy(way, half_way - 1, which).wait_recv()
            value = value + landed[way, half_way - 1, which].astype(jnp.float32)
        total[which] = value
    keep = place.x % 2
    swap[0] = total[1 - keep].astype(swap.dtype)
    swap_copy = remote(swap.at[0], swap.at[1], pair_sem.at[0], pair_sem.at[1], partner)
    start(swap_copy)
    swap_copy.wait_recv()
    piece[...] = (total[keep] + swap[1].astype(jnp.float32)).astype(piece.dtype)

    def spot(tensor, z, x):
        return out_ref.at[tensor, z * (X // 2) + x // 2, pl.ds(x % 2 * half, half)]

    here = spot(core, place.z, place.x)
    for number, z in enumerate(z_ids):
        start(remote(piece, here, z_send.at[number], z_recv.at[number], place.head_id(z, place.x, core)))
    for number, x in enumerate(x_ids):
        start(remote(piece, here, x_send.at[0, number], x_recv.at[0, number], place.head_id(place.z, x, core)))
    start(remote(piece, here, twin_send.at[0, 0], twin_recv.at[0, 0], place.sibling()))
    own = pltpu.make_async_copy(piece, here, own_sem)
    own.start()

    def landing(sem_send, sem_recv, spot_at):
        remote(spot_at, spot_at, sem_send, sem_recv, place.sibling()).wait_recv()

    for number in range(planes - 1):
        z = (place.z - number - 1 + planes) % planes
        spot_at = spot(core, z, place.x)
        landing(z_send.at[number], z_recv.at[number], spot_at)
        for index, x in enumerate(x_ids):
            start(remote(spot_at, spot_at, x_send.at[number + 1, index], x_recv.at[number + 1, index],
                         place.head_id(place.z, x, core)))
        start(remote(spot_at, spot_at, twin_send.at[number + 1, 0], twin_recv.at[number + 1, 0], place.sibling()))
    for number in range(planes):
        z = (place.z - number + planes) % planes
        for index in range(X - 1):
            x = (place.x - index - 1 + X) % X
            spot_at = spot(core, z, x)
            landing(x_send.at[number, index], x_recv.at[number, index], spot_at)
            start(remote(spot_at, spot_at, twin_send.at[number, index + 1], twin_recv.at[number, index + 1],
                         place.sibling()))
    for number in range(planes):
        z = (place.z - number + planes) % planes
        for index in range(X):
            x = (place.x - index + X) % X
            landing(twin_send.at[number, index], twin_recv.at[number, index], spot(1 - core, z, x))
    own.wait()
    for copy in started:
        copy.wait_send()


def reduce_sums(members, planes, kv_count, partial_sums):
    _, slots, _, depth = partial_sums.shape
    rows = slots // members * BLK
    half = rows // 2
    half_way = members // 2
    dma = pltpu.SemaphoreType.DMA
    low = jnp.bfloat16
    return pl.pallas_call(
        functools.partial(reduce_kernel, members, planes),
        out_shape=jax.ShapeDtypeStruct((2, kv_count, rows, depth), low),
        in_specs=[pl.BlockSpec(memory_space=pltpu.VMEM)],
        out_specs=pl.BlockSpec(memory_space=pl.ANY),
        scratch_shapes=[
            pltpu.VMEM((members, rows, depth), low),
            pltpu.VMEM((2, half_way, 2, half, depth), low),
            pltpu.VMEM((2, half_way, 2, half, depth), low),
            pltpu.VMEM((2, half, depth), jnp.float32),
            pltpu.VMEM((half, depth), low),
            pltpu.VMEM((2, half, depth), low),
            dma((members,)),
            dma((members,)),
            dma((2, half_way, 2)),
            dma((2, half_way, 2)),
            dma((2,)),
            dma,
            dma((max(planes - 1, 1),)),
            dma((max(planes - 1, 1),)),
            dma((planes, X - 1)),
            dma((planes, X - 1)),
            dma((planes, X)),
            dma((planes, X)),
        ],
        compiler_params=pltpu.CompilerParams(
            collective_id=1, has_side_effects=True, vmem_limit_bytes=VMEM_BYTES
        ),
        name="reduce_sums",
    )(partial_sums.reshape(2, members, rows, depth))


def per_device(queries, keys, values, d_out, block_pos, block_mask):
    members = lax.axis_size("ctx") // SEQS
    planes = lax.axis_size("head") // (CORES * X)
    tokens, heads, depth = queries.shape
    kv_count = keys.shape[1]
    key_all, value_all = gather(
        members, planes, jnp.transpose(keys, (1, 0, 2)), jnp.transpose(values, (1, 0, 2))
    )
    d_queries, partial_sums = local_grads(
        members,
        block_pos,
        block_mask,
        queries.reshape(tokens * heads, depth),
        d_out.reshape(tokens * heads, depth),
        key_all,
        value_all,
    )
    summed = reduce_sums(members, planes, kv_count, partial_sums)
    return (
        d_queries.reshape(tokens, heads, depth),
        jnp.transpose(summed[0], (1, 0, 2)),
        jnp.transpose(summed[1], (1, 0, 2)),
    )


def solution(mesh):
    placed = (
        P("ctx", "head", None),
        P("ctx", None, None),
        P("ctx", None, None),
        P("ctx", "head", None),
        P(),
        P(),
    )
    return jax.shard_map(
        per_device,
        mesh=mesh,
        in_specs=placed,
        out_specs=(P("ctx", "head", None), P("ctx", None, None), P("ctx", None, None)),
        check_vma=False,
    )
```

```python
import functools
import math

import jax
import jax.numpy as jnp
from jax import lax
from jax.experimental import pallas as pl
from jax.experimental.pallas import tpu as pltpu
from jax.sharding import PartitionSpec as P

GROUP = 16
BLK = 128
SEQS = 4
QB_DEV = 4
CORES = 2
X = 4
NEG = -1e30
WIDE = 8
UNROLL = 32
VMEM_BYTES = 44 * 1024 * 1024
SMALL_VMEM_BYTES = 16 * 1024 * 1024
MESH = pl.DeviceIdType.MESH


class Place:
    def __init__(self, members, planes):
        self.members = members
        self.planes = planes
        ctx = lax.axis_index("ctx")
        head = lax.axis_index("head")
        self.seq = ctx % SEQS
        self.y = ctx // SEQS
        self.core = head % CORES
        self.x = head // CORES % X
        self.z = head // (CORES * X)
        self.ctx = ctx
        self.head = head

    def member(self, steps):
        return (self.y + steps + self.members) % self.members

    def along_y(self, steps):
        return (self.member(steps) * SEQS + self.seq, self.head)

    def head_id(self, z, x, core):
        return (self.ctx, (z * X + x) * CORES + core)

    def sibling(self):
        return self.head_id(self.z, self.x, 1 - self.core)


def meet(partners):
    barrier = pltpu.get_barrier_semaphore()
    for partner in partners:
        pl.semaphore_signal(barrier, inc=1, device_id=partner, device_id_type=MESH)
    pl.semaphore_wait(barrier, len(partners))


def remote(src, dst, send_sem, recv_sem, target):
    return pltpu.make_async_remote_copy(
        src_ref=src,
        dst_ref=dst,
        send_sem=send_sem,
        recv_sem=recv_sem,
        device_id=target,
        device_id_type=MESH,
    )


def gather_kernel(members, planes, kv_per_plane, k_ref, v_ref, kg_ref, vg_ref, own_sem,
                  send_sem, recv_sem, side_send, side_recv):
    place = Place(members, planes)
    part = k_ref.shape[1] // CORES
    kv = place.z * kv_per_plane + place.x * kv_per_plane // X
    mine = pl.ds(place.core * part, part)
    other = pl.ds((1 - place.core) * part, part)
    pairs = ((k_ref, kg_ref), (v_ref, vg_ref))
    own = [
        pltpu.make_async_copy(src.at[kv], dst.at[place.y], own_sem.at[index])
        for index, (src, dst) in enumerate(pairs)
    ]
    meet([place.along_y(steps) for steps in (1, -1, 2, -2)] + [place.sibling()])
    started = []
    chains = [(tensor, way) for tensor in range(2) for way in range(2)]

    def start(copy):
        copy.start()
        started.append(copy)

    def send(tensor, way, origin, reach, steps):
        sign = 1 - 2 * way
        src_in, dst = pairs[tensor]
        at = dst.at[place.member(-sign * origin), mine]
        src = src_in.at[kv, mine] if origin == 0 else at
        start(remote(src, at, send_sem.at[tensor, way, reach - 1], recv_sem.at[tensor, way, reach - 1],
                     place.along_y(sign * steps)))

    def side_copy(tensor, way, reach, rows_at):
        at = pairs[tensor][1].at[place.member(-(1 - 2 * way) * reach), rows_at]
        return remote(at, at, side_send.at[tensor, way, reach - 1], side_recv.at[tensor, way, reach - 1],
                      place.sibling())

    def arrived(tensor, way, reach):
        at = pairs[tensor][1].at[place.member(-(1 - 2 * way) * reach), mine]
        remote(at, at, send_sem.at[tensor, way, reach - 1], recv_sem.at[tensor, way, reach - 1],
               place.sibling()).wait_recv()

    for tensor, way in chains:
        send(tensor, way, 0, 2, 2)
    for tensor, way in chains:
        send(tensor, way, 0, 1, 1)
    for copy in own:
        copy.start()
    for tensor, way in chains:
        arrived(tensor, way, 2)
        if tensor == way:
            send(tensor, way, 2, 4, 2)
        send(tensor, way, 2, 3, 1)
    steps = [(tensor, way, 2) for tensor, way in chains]
    for reach in (1, 3, 4):
        steps += [(tensor, way, reach) for tensor, way in chains if reach < 4 or tensor == way]
    for tensor, way, reach in steps:
        if reach != 2:
            arrived(tensor, way, reach)
        start(side_copy(tensor, way, reach, mine))
    for step in steps:
        side_copy(*step, other).wait_recv()
    for copy in started:
        copy.wait_send()
    for copy in own:
        copy.wait()


def gather(members, planes, keys, values):
    kv_count, rows, depth = keys.shape
    out = pltpu.VMEM((members, rows, depth), keys.dtype)
    return pl.pallas_call(
        functools.partial(gather_kernel, members, planes, kv_count // planes),
        out_shape=(out, out),
        in_specs=[pl.BlockSpec(memory_space=pl.ANY)] * 2,
        out_specs=[pl.BlockSpec(memory_space=pltpu.VMEM)] * 2,
        scratch_shapes=[pltpu.SemaphoreType.DMA((2,))]
        + [pltpu.SemaphoreType.DMA((2, 2, members // 2))] * 4,
        compiler_params=pltpu.CompilerParams(
            collective_id=0, has_side_effects=True, vmem_limit_bytes=SMALL_VMEM_BYTES
        ),
        name="gather_keys",
    )(keys, values)


def dot(left, right):
    return jnp.dot(left, right, preferred_element_type=jnp.float32)


def dot_first(left, right):
    return lax.dot_general(left, right, (((0,), (0,)), ((), ())), preferred_element_type=jnp.float32)


def grad_kernel(members, order_ref, mask_ref, q_ref, g_ref, k_ref, v_ref, dq_ref, dkv_ref,
                list_ref, exp_ref, dprob_ref, top_ref, acc_ref, dq_acc, qt_ref, gt_ref):
    ctx = lax.axis_index("ctx")
    seq = ctx % SEQS
    member = ctx // SEQS
    depth = q_ref.shape[1]
    rows = q_ref.shape[0] // QB_DEV
    heads = rows // BLK
    slots = members * QB_DEV
    scale = depth ** -0.5
    scale2 = scale * math.log2(math.e)
    acc_ref[...] = jnp.zeros_like(acc_ref)
    query_pos = [order_ref[seq, member * QB_DEV + index] for index in range(QB_DEV)]

    def list_slot(slot, counts):
        key_pos = order_ref[seq, slot]
        grown = []
        for index, count in enumerate(counts):
            list_ref[index, count] = slot
            seen = jnp.logical_and(key_pos < query_pos[index], mask_ref[seq, query_pos[index], key_pos] == 1)
            grown.append(count + seen.astype(jnp.int32))
        return tuple(grown)

    counts = lax.fori_loop(0, slots, list_slot, (jnp.int32(0),) * QB_DEV, unroll=UNROLL)
    for index, count in enumerate(counts):
        list_ref[index, slots + 1] = count

    def blocks(ref, picked):
        return jnp.concatenate([ref[slot] for slot in picked], axis=0) if len(picked) > 1 else ref[picked[0]]

    def fold(value, op):
        return op(value.reshape(value.shape[0] // 8, 8, rows), axis=0)

    def spread(value, count):
        return jnp.broadcast_to(value[None], (count // 8, 8, rows)).reshape(count, rows)

    def query_block(index, carry):
        own = member * QB_DEV + index
        count = list_ref[index, slots + 1]
        at = pl.ds(pl.multiple_of(index * rows, rows), rows)
        qt_ref[...] = q_ref[at, :].T
        gt_ref[...] = g_ref[at, :].T

        def part(start, size, body, state):
            picked = [list_ref[index, start + offset] for offset in range(size)]
            where = pl.ds(pl.multiple_of((start + 1) * BLK, BLK), size * BLK)
            return body(picked, where, start + 1, state)

        def over(body, state):
            state = lax.fori_loop(0, count // WIDE, lambda n, state: part(n * WIDE, WIDE, body, state), state)
            size = WIDE // 2
            while size:
                start = count // (2 * size) * (2 * size)
                state = lax.cond(
                    count // size % 2 == 1,
                    lambda state, start=start, size=size: part(start, size, body, state),
                    lambda state: state,
                    state,
                )
                size //= 2
            return state

        def weigh(picked, where, number, state, diagonal=False):
            maxima, totals, weighted = state
            score = dot(blocks(k_ref, picked), qt_ref[...])
            if diagonal:
                key_token = lax.broadcasted_iota(jnp.int32, (BLK, rows), 0)
                query_token = lax.broadcasted_iota(jnp.int32, (BLK, rows), 1) // heads
                score = jnp.where(key_token <= query_token, score, NEG)
            dprob = dot(blocks(v_ref, picked), gt_ref[...])
            new = jnp.maximum(maxima, fold(score, jnp.max))
            top = new * scale2
            factor = jnp.exp2(maxima * scale2 - top)
            exp_part = jnp.exp2(score * scale2 - spread(top, score.shape[0]))
            exp_ref[where, :] = exp_part
            dprob_ref[where, :] = dprob
            top_ref[number] = top
            return (
                new,
                totals * factor + fold(exp_part, jnp.sum),
                weighted * factor + fold(exp_part * dprob, jnp.sum),
            )

        zero = jnp.zeros((8, rows), jnp.float32)
        first_at = pl.ds(0, BLK)
        state = weigh([own], first_at, 0, (zero + NEG, zero, zero), True)
        maxima, totals, weighted = over(weigh, state)
        tops = maxima * scale2
        top = jnp.broadcast_to(jnp.max(tops, axis=0, keepdims=True), (8, rows))
        factor = jnp.exp2(tops - top)
        inverse = 1.0 / jnp.sum(totals * factor, axis=0, keepdims=True)
        delta = jnp.broadcast_to(jnp.sum(weighted * factor, axis=0, keepdims=True) * inverse, (8, rows))
        inverse = jnp.broadcast_to(inverse, (8, rows))

        def grads(picked, where, number, state, first=False):
            size = len(picked) * BLK
            share = jnp.exp2(top_ref[number] - top) * inverse
            prob = exp_ref[where, :] * spread(share, size)
            dscore = (prob * (dprob_ref[where, :] - spread(delta, size))).astype(jnp.bfloat16)
            key_add = dot(dscore, q_ref[at, :])
            value_add = dot(prob.astype(jnp.bfloat16), g_ref[at, :])
            for offset, slot in enumerate(picked):
                acc_ref[0, slot] += key_add[offset * BLK:(offset + 1) * BLK]
                acc_ref[1, slot] += value_add[offset * BLK:(offset + 1) * BLK]
            add = dot_first(dscore, blocks(k_ref, picked))
            dq_acc[...] = add if first else dq_acc[...] + add
            return state

        grads([own], first_at, 0, 0, True)
        over(grads, 0)
        dq_ref[at, :] = (dq_acc[...] * scale).astype(dq_ref.dtype)
        return carry

    lax.fori_loop(0, QB_DEV, query_block, 0)
    dkv_ref[0] = (acc_ref[0] * scale).astype(dkv_ref.dtype)
    dkv_ref[1] = acc_ref[1].astype(dkv_ref.dtype)


def local_grads(members, block_pos, block_mask, query_rows, grad_rows, keys, values):
    row_total, depth = query_rows.shape
    slots = members * QB_DEV
    rows = row_total // QB_DEV
    smem = pl.BlockSpec(memory_space=pltpu.SMEM)
    vmem = pl.BlockSpec(memory_space=pltpu.VMEM)
    return pl.pallas_call(
        functools.partial(grad_kernel, members),
        out_shape=(
            jax.ShapeDtypeStruct((row_total, depth), jnp.bfloat16),
            pltpu.VMEM((2, slots, BLK, depth), jnp.bfloat16),
        ),
        in_specs=[smem, smem, vmem, vmem, vmem, vmem],
        out_specs=(vmem, vmem),
        scratch_shapes=[
            pltpu.SMEM((QB_DEV, slots + 2), jnp.int32),
            pltpu.VMEM((slots * BLK, rows), jnp.float32),
            pltpu.VMEM((slots * BLK, rows), jnp.float32),
            pltpu.VMEM((slots, 8, rows), jnp.float32),
            pltpu.VMEM((2, slots, BLK, depth), jnp.float32),
            pltpu.VMEM((rows, depth), jnp.float32),
            pltpu.VMEM((depth, rows), jnp.bfloat16),
            pltpu.VMEM((depth, rows), jnp.bfloat16),
        ],
        compiler_params=pltpu.CompilerParams(vmem_limit_bytes=VMEM_BYTES),
        name="local_grads",
    )(block_pos, block_mask, query_rows, grad_rows,
      keys.reshape(slots, BLK, depth), values.reshape(slots, BLK, depth))


def reduce_kernel(members, planes, part_ref, out_ref, side, sums, landed, piece, swap,
                  side_send, side_recv, ring_send, ring_recv, pair_sem, own_sem,
                  z_send, z_recv, x_send, x_recv, twin_send, twin_recv):
    place = Place(members, planes)
    rows = part_ref.shape[2]
    half = rows // 2
    core = place.core
    pair_x = place.x + 1 - 2 * (place.x % 2)
    partner = place.head_id(place.z, pair_x, core)
    z_ids = [(place.z + step) % planes for step in range(1, planes)]
    x_ids = [(place.x + step) % X for step in range(1, X)]
    meet(
        [place.sibling()]
        + [place.along_y(steps) for steps in (1, -1, 2, -2)]
        + [place.head_id(place.z, x, core) for x in x_ids]
        + [place.head_id(z, place.x, core) for z in z_ids]
    )
    started = []

    def start(copy):
        copy.start()
        started.append(copy)

    offsets = [4, 3, -3, 1, -1, 2, -2, 0]

    def side_copy(steps):
        at = place.member(steps)
        slot = offsets.index(steps)
        return remote(part_ref.at[1 - core, at], side.at[slot], side_send.at[slot], side_recv.at[slot], place.sibling())

    for steps in offsets:
        start(side_copy(steps))

    def base(steps, which):
        slot = offsets.index(steps)
        at = place.member(steps)
        rows_at = pl.ds(which * half, half)
        return (part_ref[core, at, rows_at, :].astype(jnp.float32)
                + side[slot, rows_at, :].astype(jnp.float32))

    def ring_copy(way, reach, which, steps):
        return remote(
            sums.at[way, reach - 1, which],
            landed.at[way, reach - 1, which],
            ring_send.at[way, reach - 1, which],
            ring_recv.at[way, reach - 1, which],
            place.along_y((1 - 2 * way) * steps),
        )

    def arrived(way, reach, which):
        ring_copy(way, reach, which, 1).wait_recv()
        return landed[way, reach - 1, which].astype(jnp.float32)

    def send(way, reach, which, steps, value):
        sums[way, reach - 1, which] = value.astype(sums.dtype)
        start(ring_copy(way, reach, which, steps))

    def owner(way, reach):
        return 4 if reach == 4 else (1 - 2 * way) * reach

    side_copy(4).wait_recv()
    for way in range(2):
        send(way, 4, way, 2, base(4, way))
    for reach in (3, 1):
        for way in range(2):
            side_copy(owner(way, reach)).wait_recv()
            for which in range(2):
                send(way, reach, which, 1, base(owner(way, reach), which))
    for way in range(2):
        side_copy(owner(way, 2)).wait_recv()
        send(way, 2, 1 - way, 2, base(owner(way, 2), 1 - way) + arrived(way, 3, 1 - way))
    for way in range(2):
        send(way, 2, way, 2, base(owner(way, 2), way) + arrived(way, 3, way) + arrived(way, 4, way))
    side_copy(0).wait_recv()
    keep = place.x % 2

    for way in range(2):
        for reach in (1, 2):
            for which in range(2):
                ring_copy(way, reach, which, 1).wait_recv()

    def total(which):
        value = base(0, which)
        for way in range(2):
            for reach in (1, 2):
                value = value + landed[way, reach - 1, which].astype(jnp.float32)
        return value

    swap[0] = total(1 - keep).astype(swap.dtype)
    swap_copy = remote(swap.at[0], swap.at[1], pair_sem.at[0], pair_sem.at[1], partner)
    start(swap_copy)
    kept = total(keep)
    swap_copy.wait_recv()
    piece[...] = (kept + swap[1].astype(jnp.float32)).astype(piece.dtype)

    def spot(tensor, z, x):
        return out_ref.at[tensor, z * (X // 2) + x // 2, pl.ds(x % 2 * half, half)]

    here = spot(core, place.z, place.x)
    for number, z in enumerate(z_ids):
        start(remote(piece, here, z_send.at[number], z_recv.at[number], place.head_id(z, place.x, core)))
    for number, x in enumerate(x_ids):
        start(remote(piece, here, x_send.at[0, number], x_recv.at[0, number], place.head_id(place.z, x, core)))
    start(remote(piece, here, twin_send.at[0, 0], twin_recv.at[0, 0], place.sibling()))
    own = pltpu.make_async_copy(piece, here, own_sem)
    own.start()

    def landing(sem_send, sem_recv, spot_at):
        remote(spot_at, spot_at, sem_send, sem_recv, place.sibling()).wait_recv()

    def pass_on(number, index, x):
        spot_at = spot(core, (place.z - number + planes) % planes, x)
        landing(x_send.at[number, index], x_recv.at[number, index], spot_at)
        start(remote(spot_at, spot_at, twin_send.at[number, index + 1], twin_recv.at[number, index + 1],
                     place.sibling()))

    for number in range(planes - 1):
        z = (place.z - number - 1 + planes) % planes
        spot_at = spot(core, z, place.x)
        landing(z_send.at[number], z_recv.at[number], spot_at)
        for index, x in enumerate(x_ids):
            start(remote(spot_at, spot_at, x_send.at[number + 1, index], x_recv.at[number + 1, index],
                         place.head_id(place.z, x, core)))
        start(remote(spot_at, spot_at, twin_send.at[number + 1, 0], twin_recv.at[number + 1, 0], place.sibling()))
    for number in range(planes):
        for index in range(X - 1):
            pass_on(number, index, (place.x - index - 1 + X) % X)
    for number in range(planes):
        z = (place.z - number + planes) % planes
        for index in range(X):
            x = (place.x - index + X) % X
            landing(twin_send.at[number, index], twin_recv.at[number, index], spot(1 - core, z, x))
    own.wait()
    for copy in started:
        copy.wait_send()


def reduce_sums(members, planes, kv_count, partial_sums):
    _, slots, _, depth = partial_sums.shape
    rows = slots // members * BLK
    half = rows // 2
    dma = pltpu.SemaphoreType.DMA
    low = jnp.bfloat16
    return pl.pallas_call(
        functools.partial(reduce_kernel, members, planes),
        out_shape=pltpu.VMEM((2, kv_count, rows, depth), low),
        in_specs=[pl.BlockSpec(memory_space=pltpu.VMEM)],
        out_specs=pl.BlockSpec(memory_space=pltpu.VMEM),
        scratch_shapes=[
            pltpu.VMEM((members, rows, depth), low),
            pltpu.VMEM((2, 4, 2, half, depth), low),
            pltpu.VMEM((2, 4, 2, half, depth), low),
            pltpu.VMEM((half, depth), low),
            pltpu.VMEM((2, half, depth), low),
            dma((members,)),
            dma((members,)),
            dma((2, 4, 2)),
            dma((2, 4, 2)),
            dma((2,)),
            dma,
            dma((max(planes - 1, 1),)),
            dma((max(planes - 1, 1),)),
            dma((planes, X - 1)),
            dma((planes, X - 1)),
            dma((planes, X)),
            dma((planes, X)),
        ],
        compiler_params=pltpu.CompilerParams(
            collective_id=1, has_side_effects=True, vmem_limit_bytes=SMALL_VMEM_BYTES
        ),
        name="reduce_sums",
    )(partial_sums.reshape(2, members, rows, depth))


def per_device(queries, keys, values, d_out, block_pos, block_mask):
    members = lax.axis_size("ctx") // SEQS
    planes = lax.axis_size("head") // (CORES * X)
    tokens, heads, depth = queries.shape
    kv_count = keys.shape[1]
    key_all, value_all = gather(
        members, planes, jnp.transpose(keys, (1, 0, 2)), jnp.transpose(values, (1, 0, 2))
    )
    d_queries, partial_sums = local_grads(
        members,
        block_pos,
        block_mask,
        queries.reshape(tokens * heads, depth),
        d_out.reshape(tokens * heads, depth),
        key_all,
        value_all,
    )
    summed = reduce_sums(members, planes, kv_count, partial_sums)
    return (
        d_queries.reshape(tokens, heads, depth),
        jnp.transpose(summed[0], (1, 0, 2)),
        jnp.transpose(summed[1], (1, 0, 2)),
    )


def solution(mesh):
    placed = (
        P("ctx", "head", None),
        P("ctx", None, None),
        P("ctx", None, None),
        P("ctx", "head", None),
        P(),
        P(),
    )
    return jax.shard_map(
        per_device,
        mesh=mesh,
        in_specs=placed,
        out_specs=(P("ctx", "head", None), P("ctx", None, None), P("ctx", None, None)),
        check_vma=False,
    )
```

```python
import functools
import math

import jax
import jax.numpy as jnp
from jax import lax
from jax.experimental import pallas as pl
from jax.experimental.pallas import tpu as pltpu
from jax.sharding import PartitionSpec as P

GROUP = 16
BLK = 128
SEQS = 4
QB_DEV = 4
CORES = 2
X = 4
NEG = -1e30
WIDE = 8
UNROLL = 32
VMEM_BYTES = 44 * 1024 * 1024
SMALL_VMEM_BYTES = 16 * 1024 * 1024
MESH = pl.DeviceIdType.MESH


class Place:
    def __init__(self, members, planes):
        self.members = members
        self.planes = planes
        ctx = lax.axis_index("ctx")
        head = lax.axis_index("head")
        self.seq = ctx % SEQS
        self.y = ctx // SEQS
        self.core = head % CORES
        self.x = head // CORES % X
        self.z = head // (CORES * X)
        self.ctx = ctx
        self.head = head

    def member(self, steps):
        return (self.y + steps + self.members) % self.members

    def along_y(self, steps):
        return (self.member(steps) * SEQS + self.seq, self.head)

    def head_id(self, z, x, core):
        return (self.ctx, (z * X + x) * CORES + core)

    def sibling(self):
        return self.head_id(self.z, self.x, 1 - self.core)


def meet(partners):
    barrier = pltpu.get_barrier_semaphore()
    for partner in partners:
        pl.semaphore_signal(barrier, inc=1, device_id=partner, device_id_type=MESH)
    pl.semaphore_wait(barrier, len(partners))


def remote(src, dst, send_sem, recv_sem, target):
    return pltpu.make_async_remote_copy(
        src_ref=src,
        dst_ref=dst,
        send_sem=send_sem,
        recv_sem=recv_sem,
        device_id=target,
        device_id_type=MESH,
    )


def gather_kernel(members, planes, kv_per_plane, k_ref, v_ref, kg_ref, vg_ref, own_sem,
                  send_sem, recv_sem, side_send, side_recv):
    place = Place(members, planes)
    part = k_ref.shape[1] // CORES
    kv = place.z * kv_per_plane + place.x * kv_per_plane // X
    mine = pl.ds(place.core * part, part)
    other = pl.ds((1 - place.core) * part, part)
    pairs = ((k_ref, kg_ref), (v_ref, vg_ref))
    own = [
        pltpu.make_async_copy(src.at[kv], dst.at[place.y], own_sem.at[index])
        for index, (src, dst) in enumerate(pairs)
    ]
    meet([place.along_y(steps) for steps in (1, -1, 2, -2)] + [place.sibling()])
    started = []
    chains = [(tensor, way) for tensor in range(2) for way in range(2)]

    def start(copy):
        copy.start()
        started.append(copy)

    def send(tensor, way, origin, reach, steps):
        sign = 1 - 2 * way
        src_in, dst = pairs[tensor]
        at = dst.at[place.member(-sign * origin), mine]
        src = src_in.at[kv, mine] if origin == 0 else at
        start(remote(src, at, send_sem.at[tensor, way, reach - 1], recv_sem.at[tensor, way, reach - 1],
                     place.along_y(sign * steps)))

    def side_copy(tensor, way, reach, rows_at):
        at = pairs[tensor][1].at[place.member(-(1 - 2 * way) * reach), rows_at]
        return remote(at, at, side_send.at[tensor, way, reach - 1], side_recv.at[tensor, way, reach - 1],
                      place.sibling())

    def arrived(tensor, way, reach):
        at = pairs[tensor][1].at[place.member(-(1 - 2 * way) * reach), mine]
        remote(at, at, send_sem.at[tensor, way, reach - 1], recv_sem.at[tensor, way, reach - 1],
               place.sibling()).wait_recv()

    for tensor, way in chains:
        send(tensor, way, 0, 2, 2)
    for tensor, way in chains:
        send(tensor, way, 0, 1, 1)
    for copy in own:
        copy.start()
    for tensor, way in chains:
        arrived(tensor, way, 2)
        if tensor == way:
            send(tensor, way, 2, 4, 2)
        send(tensor, way, 2, 3, 1)
    steps = [(tensor, way, 2) for tensor, way in chains]
    for reach in (1, 3, 4):
        steps += [(tensor, way, reach) for tensor, way in chains if reach < 4 or tensor == way]
    for tensor, way, reach in steps:
        if reach != 2:
            arrived(tensor, way, reach)
        start(side_copy(tensor, way, reach, mine))
    for step in steps:
        side_copy(*step, other).wait_recv()
    for copy in started:
        copy.wait_send()
    for copy in own:
        copy.wait()


def gather(members, planes, keys, values):
    kv_count, rows, depth = keys.shape
    out = pltpu.VMEM((members, rows, depth), keys.dtype)
    return pl.pallas_call(
        functools.partial(gather_kernel, members, planes, kv_count // planes),
        out_shape=(out, out),
        in_specs=[pl.BlockSpec(memory_space=pltpu.HBM)] * 2,
        out_specs=[pl.BlockSpec(memory_space=pltpu.VMEM)] * 2,
        scratch_shapes=[pltpu.SemaphoreType.DMA((2,))]
        + [pltpu.SemaphoreType.DMA((2, 2, members // 2))] * 4,
        compiler_params=pltpu.CompilerParams(
            collective_id=0, has_side_effects=True, vmem_limit_bytes=SMALL_VMEM_BYTES
        ),
        name="gather_keys",
    )(pltpu.with_memory_space_constraint(keys, pltpu.HBM), pltpu.with_memory_space_constraint(values, pltpu.HBM))


def dot(left, right):
    return jnp.dot(left, right, preferred_element_type=jnp.float32)


def dot_first(left, right):
    return lax.dot_general(left, right, (((0,), (0,)), ((), ())), preferred_element_type=jnp.float32)


def grad_kernel(members, order_ref, mask_ref, q_ref, g_ref, k_ref, v_ref, dq_ref, dkv_ref,
                list_ref, exp_ref, dprob_ref, top_ref, acc_ref, dq_acc, qt_ref, gt_ref):
    ctx = lax.axis_index("ctx")
    seq = ctx % SEQS
    member = ctx // SEQS
    depth = q_ref.shape[1]
    rows = q_ref.shape[0] // QB_DEV
    heads = rows // BLK
    slots = members * QB_DEV
    scale = depth ** -0.5
    scale2 = scale * math.log2(math.e)
    acc_ref[...] = jnp.zeros_like(acc_ref)
    query_pos = [order_ref[seq, member * QB_DEV + index] for index in range(QB_DEV)]

    def list_slot(slot, counts):
        key_pos = order_ref[seq, slot]
        grown = []
        for index, count in enumerate(counts):
            list_ref[index, count] = slot
            seen = jnp.logical_and(key_pos < query_pos[index], mask_ref[seq, query_pos[index], key_pos] == 1)
            grown.append(count + seen.astype(jnp.int32))
        return tuple(grown)

    counts = lax.fori_loop(0, slots, list_slot, (jnp.int32(0),) * QB_DEV, unroll=UNROLL)
    for index, count in enumerate(counts):
        list_ref[index, slots + 1] = count

    def blocks(ref, picked):
        return jnp.concatenate([ref[slot] for slot in picked], axis=0) if len(picked) > 1 else ref[picked[0]]

    def fold(value, op):
        return op(value.reshape(value.shape[0] // 8, 8, rows), axis=0)

    def spread(value, count):
        return jnp.broadcast_to(value[None], (count // 8, 8, rows)).reshape(count, rows)

    def query_block(index, carry):
        own = member * QB_DEV + index
        count = list_ref[index, slots + 1]
        at = pl.ds(pl.multiple_of(index * rows, rows), rows)
        qt_ref[...] = q_ref[at, :].T
        gt_ref[...] = g_ref[at, :].T

        def part(start, size, body, state):
            picked = [list_ref[index, start + offset] for offset in range(size)]
            where = pl.ds(pl.multiple_of((start + 1) * BLK, BLK), size * BLK)
            return body(picked, where, start + 1, state)

        def over(body, state):
            state = lax.fori_loop(0, count // WIDE, lambda n, state: part(n * WIDE, WIDE, body, state), state)
            size = WIDE // 2
            while size:
                start = count // (2 * size) * (2 * size)
                state = lax.cond(
                    count // size % 2 == 1,
                    lambda state, start=start, size=size: part(start, size, body, state),
                    lambda state: state,
                    state,
                )
                size //= 2
            return state

        def weigh(picked, where, number, state, diagonal=False):
            maxima, totals, weighted = state
            score = dot(blocks(k_ref, picked), qt_ref[...])
            if diagonal:
                key_token = lax.broadcasted_iota(jnp.int32, (BLK, rows), 0)
                query_token = lax.broadcasted_iota(jnp.int32, (BLK, rows), 1) // heads
                score = jnp.where(key_token <= query_token, score, NEG)
            dprob = dot(blocks(v_ref, picked), gt_ref[...])
            new = jnp.maximum(maxima, fold(score, jnp.max))
            top = new * scale2
            factor = jnp.exp2(maxima * scale2 - top)
            exp_part = jnp.exp2(score * scale2 - spread(top, score.shape[0]))
            exp_ref[where, :] = exp_part
            dprob_ref[where, :] = dprob
            top_ref[number] = top
            return (
                new,
                totals * factor + fold(exp_part, jnp.sum),
                weighted * factor + fold(exp_part * dprob, jnp.sum),
            )

        zero = jnp.zeros((8, rows), jnp.float32)
        first_at = pl.ds(0, BLK)
        state = weigh([own], first_at, 0, (zero + NEG, zero, zero), True)
        maxima, totals, weighted = over(weigh, state)
        tops = maxima * scale2
        top = jnp.broadcast_to(jnp.max(tops, axis=0, keepdims=True), (8, rows))
        factor = jnp.exp2(tops - top)
        inverse = 1.0 / jnp.sum(totals * factor, axis=0, keepdims=True)
        delta = jnp.broadcast_to(jnp.sum(weighted * factor, axis=0, keepdims=True) * inverse, (8, rows))
        inverse = jnp.broadcast_to(inverse, (8, rows))

        def grads(picked, where, number, state, first=False):
            size = len(picked) * BLK
            share = jnp.exp2(top_ref[number] - top) * inverse
            prob = exp_ref[where, :] * spread(share, size)
            dscore = (prob * (dprob_ref[where, :] - spread(delta, size))).astype(jnp.bfloat16)
            key_add = dot(dscore, q_ref[at, :])
            value_add = dot(prob.astype(jnp.bfloat16), g_ref[at, :])
            for offset, slot in enumerate(picked):
                acc_ref[0, slot] += key_add[offset * BLK:(offset + 1) * BLK]
                acc_ref[1, slot] += value_add[offset * BLK:(offset + 1) * BLK]
            add = dot_first(dscore, blocks(k_ref, picked))
            dq_acc[...] = add if first else dq_acc[...] + add
            return state

        grads([own], first_at, 0, 0, True)
        over(grads, 0)
        dq_ref[at, :] = (dq_acc[...] * scale).astype(dq_ref.dtype)
        return carry

    lax.fori_loop(0, QB_DEV, query_block, 0)
    dkv_ref[0] = (acc_ref[0] * scale).astype(dkv_ref.dtype)
    dkv_ref[1] = acc_ref[1].astype(dkv_ref.dtype)


def local_grads(members, block_pos, block_mask, query_rows, grad_rows, keys, values):
    row_total, depth = query_rows.shape
    slots = members * QB_DEV
    rows = row_total // QB_DEV
    smem = pl.BlockSpec(memory_space=pltpu.SMEM)
    vmem = pl.BlockSpec(memory_space=pltpu.VMEM)
    return pl.pallas_call(
        functools.partial(grad_kernel, members),
        out_shape=(
            jax.ShapeDtypeStruct((row_total, depth), jnp.bfloat16),
            pltpu.VMEM((2, slots, BLK, depth), jnp.bfloat16),
        ),
        in_specs=[smem, smem, vmem, vmem, vmem, vmem],
        out_specs=(vmem, vmem),
        scratch_shapes=[
            pltpu.SMEM((QB_DEV, slots + 2), jnp.int32),
            pltpu.VMEM((slots * BLK, rows), jnp.float32),
            pltpu.VMEM((slots * BLK, rows), jnp.float32),
            pltpu.VMEM((slots, 8, rows), jnp.float32),
            pltpu.VMEM((2, slots, BLK, depth), jnp.float32),
            pltpu.VMEM((rows, depth), jnp.float32),
            pltpu.VMEM((depth, rows), jnp.bfloat16),
            pltpu.VMEM((depth, rows), jnp.bfloat16),
        ],
        compiler_params=pltpu.CompilerParams(vmem_limit_bytes=VMEM_BYTES),
        name="local_grads",
    )(block_pos, block_mask, query_rows, grad_rows,
      keys.reshape(slots, BLK, depth), values.reshape(slots, BLK, depth))


def reduce_kernel(members, planes, part_ref, out_ref, side, give, given, sums, landed, piece,
                  side_send, side_recv, pair_send, pair_recv, ring_send, ring_recv, own_sem,
                  z_send, z_recv, x_send, x_recv, twin_send, twin_recv):
    place = Place(members, planes)
    half = part_ref.shape[2] // 2
    quarter = half // 2
    core = place.core
    keep = place.x % 2
    partner = place.head_id(place.z, place.x + 1 - 2 * keep, core)
    z_ids = [(place.z + step) % planes for step in range(1, planes)]
    x_ids = [(place.x + step) % X for step in range(1, X)]
    meet(
        [place.sibling()]
        + [place.along_y(steps) for steps in (1, -1, 2, -2)]
        + [place.head_id(place.z, x, core) for x in x_ids]
        + [place.head_id(z, place.x, core) for z in z_ids]
    )
    started = []

    def start(copy):
        copy.start()
        started.append(copy)

    offsets = [4, 3, -3, 1, -1, 2, -2, 0]

    def side_copy(steps):
        at = place.member(steps)
        slot = offsets.index(steps)
        return remote(part_ref.at[1 - core, at], side.at[slot], side_send.at[slot], side_recv.at[slot], place.sibling())

    def pair_copy(steps):
        slot = offsets.index(steps)
        return remote(give.at[slot], given.at[slot], pair_send.at[slot], pair_recv.at[slot], partner)

    def chip_sum(steps, which):
        rows_at = pl.ds(pl.multiple_of(which * half, half), half)
        return (part_ref[core, place.member(steps), rows_at, :].astype(jnp.float32)
                + side[offsets.index(steps), rows_at, :].astype(jnp.float32))

    def pair_sum(steps):
        pair_copy(steps).wait_recv()
        return chip_sum(steps, keep) + given[offsets.index(steps)].astype(jnp.float32)

    def ring_copy(way, reach, steps):
        rows_at = pl.ds(way * quarter, quarter) if reach == 4 else pl.ds(0, half)
        return remote(
            sums.at[way, reach - 1, rows_at],
            landed.at[way, reach - 1, rows_at],
            ring_send.at[way, reach - 1],
            ring_recv.at[way, reach - 1],
            place.along_y((1 - 2 * way) * steps),
        )

    def send(way, reach, steps, value):
        sums[way, reach - 1] = value.astype(sums.dtype)
        start(ring_copy(way, reach, steps))

    for steps in offsets:
        start(side_copy(steps))
    for steps in offsets:
        side_copy(steps).wait_recv()
        give[offsets.index(steps)] = chip_sum(steps, 1 - keep).astype(give.dtype)
        start(pair_copy(steps))
    far = pair_sum(4)
    for way in range(2):
        send(way, 4, 2, far)
    for reach in (3, 1):
        for way in range(2):
            send(way, reach, 1, pair_sum((1 - 2 * way) * reach))
    for way in range(2):
        value = pair_sum((1 - 2 * way) * 2)
        ring_copy(way, 3, 1).wait_recv()
        value = value + landed[way, 2].astype(jnp.float32)
        ring_copy(way, 4, 2).wait_recv()
        late = value[way * quarter:(way + 1) * quarter] + landed[
            way, 3, way * quarter:(way + 1) * quarter].astype(jnp.float32)
        early = value[(1 - way) * quarter:(2 - way) * quarter]
        send(way, 2, 2, jnp.concatenate([early, late] if way else [late, early], axis=0))
    value = pair_sum(0)
    for reach in (1, 2):
        for way in range(2):
            ring_copy(way, reach, 1).wait_recv()
            value = value + landed[way, reach - 1].astype(jnp.float32)
    piece[...] = value.astype(piece.dtype)

    def spot(tensor, z, x, sub=None):
        start_at, size = (0, half) if sub is None else (sub * quarter, quarter)
        rows_at = pl.ds(pl.multiple_of(x % 2 * half + start_at, size), size)
        return out_ref.at[tensor, z * (X // 2) + x // 2, rows_at]

    here = spot(core, place.z, place.x)
    for sub in range(2):
        for number, z in enumerate(z_ids):
            start(remote(piece.at[pl.ds(sub * quarter, quarter)], spot(core, place.z, place.x, sub),
                         z_send.at[number, sub], z_recv.at[number, sub], place.head_id(z, place.x, core)))
    for number, x in enumerate(x_ids):
        start(remote(piece, here, x_send.at[0, number, 0], x_recv.at[0, number, 0], place.head_id(place.z, x, core)))
    start(remote(piece, here, twin_send.at[0, 0], twin_recv.at[0, 0], place.sibling()))
    own = pltpu.make_async_copy(piece, here, own_sem)
    own.start()

    def landing(sem_send, sem_recv, spot_at):
        remote(spot_at, spot_at, sem_send, sem_recv, place.sibling()).wait_recv()

    def from_plane(number):
        return (place.z - number + planes) % planes

    def to_twin(number, index, x):
        spot_at = spot(core, from_plane(number), x)
        start(remote(spot_at, spot_at, twin_send.at[number, index], twin_recv.at[number, index], place.sibling()))

    for sub in range(2):
        for number in range(1, planes):
            spot_at = spot(core, from_plane(number), place.x, sub)
            landing(z_send.at[number - 1, sub], z_recv.at[number - 1, sub], spot_at)
            for index, x in enumerate(x_ids):
                start(remote(spot_at, spot_at, x_send.at[number, index, sub], x_recv.at[number, index, sub],
                             place.head_id(place.z, x, core)))
    for number in range(1, planes):
        to_twin(number, 0, place.x)
    for number in range(planes):
        for index in range(X - 1):
            x = (place.x - index - 1 + X) % X
            for sub in range(2) if number else (None,):
                landing(x_send.at[number, index, sub or 0], x_recv.at[number, index, sub or 0],
                        spot(core, from_plane(number), x, sub))
            to_twin(number, index + 1, x)
    for number in range(planes):
        for index in range(X):
            x = (place.x - index + X) % X
            landing(twin_send.at[number, index], twin_recv.at[number, index], spot(1 - core, from_plane(number), x))
    own.wait()
    for copy in started:
        copy.wait_send()


def reduce_sums(members, planes, kv_count, partial_sums):
    _, slots, _, depth = partial_sums.shape
    rows = slots // members * BLK
    half = rows // 2
    dma = pltpu.SemaphoreType.DMA
    low = jnp.bfloat16
    z_count = max(planes - 1, 1)
    return pl.pallas_call(
        functools.partial(reduce_kernel, members, planes),
        out_shape=pltpu.VMEM((2, kv_count, rows, depth), low),
        in_specs=[pl.BlockSpec(memory_space=pltpu.VMEM)],
        out_specs=pl.BlockSpec(memory_space=pltpu.VMEM),
        scratch_shapes=[
            pltpu.VMEM((members, rows, depth), low),
            pltpu.VMEM((members, half, depth), low),
            pltpu.VMEM((members, half, depth), low),
            pltpu.VMEM((2, 4, half, depth), low),
            pltpu.VMEM((2, 4, half, depth), low),
            pltpu.VMEM((half, depth), low),
            dma((members,)),
            dma((members,)),
            dma((members,)),
            dma((members,)),
            dma((2, 4)),
            dma((2, 4)),
            dma,
            dma((z_count, 2)),
            dma((z_count, 2)),
            dma((planes, X - 1, 2)),
            dma((planes, X - 1, 2)),
            dma((planes, X)),
            dma((planes, X)),
        ],
        compiler_params=pltpu.CompilerParams(
            collective_id=1, has_side_effects=True, vmem_limit_bytes=SMALL_VMEM_BYTES
        ),
        name="reduce_sums",
    )(partial_sums.reshape(2, members, rows, depth))


def per_device(queries, keys, values, d_out, block_pos, block_mask):
    members = lax.axis_size("ctx") // SEQS
    planes = lax.axis_size("head") // (CORES * X)
    tokens, heads, depth = queries.shape
    kv_count = keys.shape[1]
    key_all, value_all = gather(
        members, planes, jnp.transpose(keys, (1, 0, 2)), jnp.transpose(values, (1, 0, 2))
    )
    d_queries, partial_sums = local_grads(
        members,
        block_pos,
        block_mask,
        queries.reshape(tokens * heads, depth),
        d_out.reshape(tokens * heads, depth),
        key_all,
        value_all,
    )
    summed = reduce_sums(members, planes, kv_count, partial_sums)
    return (
        d_queries.reshape(tokens, heads, depth),
        jnp.transpose(summed[0], (1, 0, 2)),
        jnp.transpose(summed[1], (1, 0, 2)),
    )


def solution(mesh):
    placed = (
        P("ctx", "head", None),
        P("ctx", None, None),
        P("ctx", None, None),
        P("ctx", "head", None),
        P(),
        P(),
    )
    return jax.shard_map(
        per_device,
        mesh=mesh,
        in_specs=placed,
        out_specs=(P("ctx", "head", None), P("ctx", None, None), P("ctx", None, None)),
        check_vma=False,
    )
```

```python
import functools
import math

import jax
import jax.numpy as jnp
from jax import lax
from jax.experimental import pallas as pl
from jax.experimental.pallas import tpu as pltpu
from jax.sharding import PartitionSpec as P

GROUP = 16
BLK = 128
SEQS = 4
QB_DEV = 4
CORES = 2
X = 4
NEG = -1e30
WIDE = 8
UNROLL = 32
VMEM_BYTES = 44 * 1024 * 1024
SMALL_VMEM_BYTES = 16 * 1024 * 1024
MESH = pl.DeviceIdType.MESH


class Place:
    def __init__(self, members, planes):
        self.members = members
        self.planes = planes
        ctx = lax.axis_index("ctx")
        head = lax.axis_index("head")
        self.seq = ctx % SEQS
        self.y = ctx // SEQS
        self.core = head % CORES
        self.x = head // CORES % X
        self.z = head // (CORES * X)
        self.ctx = ctx
        self.head = head

    def member(self, steps):
        return (self.y + steps + self.members) % self.members

    def along_y(self, steps):
        return (self.member(steps) * SEQS + self.seq, self.head)

    def head_id(self, z, x, core):
        return (self.ctx, (z * X + x) * CORES + core)

    def sibling(self):
        return self.head_id(self.z, self.x, 1 - self.core)


def meet(partners):
    barrier = pltpu.get_barrier_semaphore()
    for partner in partners:
        pl.semaphore_signal(barrier, inc=1, device_id=partner, device_id_type=MESH)
    pl.semaphore_wait(barrier, len(partners))


def remote(src, dst, send_sem, recv_sem, target):
    return pltpu.make_async_remote_copy(
        src_ref=src,
        dst_ref=dst,
        send_sem=send_sem,
        recv_sem=recv_sem,
        device_id=target,
        device_id_type=MESH,
    )


def gather_kernel(members, planes, kv_per_plane, k_ref, v_ref, kg_ref, vg_ref, own_sem,
                  send_sem, recv_sem, pair_send, pair_recv, side_send, side_recv):
    place = Place(members, planes)
    part = k_ref.shape[1] // CORES
    quarter = part // 2
    kv = place.z * kv_per_plane + place.x * kv_per_plane // X
    lane = place.x % 2
    partner = place.head_id(place.z, place.x + 1 - 2 * lane, place.core)
    mine = pl.ds(pl.multiple_of(place.core * part, part), part)
    other = pl.ds(pl.multiple_of((1 - place.core) * part, part), part)
    kept = pl.ds(pl.multiple_of(place.core * part + lane * quarter, quarter), quarter)
    lacked = pl.ds(pl.multiple_of(place.core * part + (1 - lane) * quarter, quarter), quarter)
    pairs = ((k_ref, kg_ref), (v_ref, vg_ref))
    own = [
        pltpu.make_async_copy(src.at[kv], dst.at[place.y], own_sem.at[index])
        for index, (src, dst) in enumerate(pairs)
    ]
    meet([place.along_y(steps) for steps in (1, -1, 2, -2)] + [partner, place.sibling()])
    started = []
    chains = [(tensor, way) for tensor in range(2) for way in range(2)]

    def start(copy):
        copy.start()
        started.append(copy)

    def rows_of(reach):
        return mine if reach == 1 else kept

    def slab(tensor, way, reach, rows_at):
        return pairs[tensor][1].at[place.member(-(1 - 2 * way) * reach), rows_at]

    def send(tensor, way, origin, reach, steps):
        sign = 1 - 2 * way
        src_in, dst = pairs[tensor]
        at = dst.at[place.member(-sign * origin), rows_of(reach)]
        src = src_in.at[kv, rows_of(reach)] if origin == 0 else at
        start(remote(src, at, send_sem.at[tensor, way, reach - 1], recv_sem.at[tensor, way, reach - 1],
                     place.along_y(sign * steps)))

    def arrived(tensor, way, reach):
        at = slab(tensor, way, reach, rows_of(reach))
        remote(at, at, send_sem.at[tensor, way, reach - 1], recv_sem.at[tensor, way, reach - 1],
               place.sibling()).wait_recv()

    def pair_copy(tensor, way, reach, rows_at):
        at = slab(tensor, way, reach, rows_at)
        return remote(at, at, pair_send.at[tensor, way, reach - 1], pair_recv.at[tensor, way, reach - 1], partner)

    def side_copy(tensor, way, reach, rows_at):
        at = slab(tensor, way, reach, rows_at)
        return remote(at, at, side_send.at[tensor, way, reach - 1], side_recv.at[tensor, way, reach - 1],
                      place.sibling())

    for tensor, way in chains:
        send(tensor, way, 0, 2, 2)
    for tensor, way in chains:
        send(tensor, way, 0, 1, 1)
    for copy in own:
        copy.start()
    for tensor, way in chains:
        arrived(tensor, way, 2)
        if tensor == way:
            send(tensor, way, 2, 4, 2)
        send(tensor, way, 2, 3, 1)
        start(pair_copy(tensor, way, 2, kept))
    for tensor, way in chains:
        arrived(tensor, way, 1)
        start(side_copy(tensor, way, 1, mine))
    far = [(tensor, way, 3) for tensor, way in chains] + [(tensor, way, 4) for tensor, way in chains if tensor == way]
    for tensor, way, reach in far:
        arrived(tensor, way, reach)
        start(pair_copy(tensor, way, reach, kept))
    far = [(tensor, way, 2) for tensor, way in chains] + far
    for step in far:
        pair_copy(*step, lacked).wait_recv()
        start(side_copy(*step, mine))
    for step in [(tensor, way, 1) for tensor, way in chains] + far:
        side_copy(*step, other).wait_recv()
    for copy in started:
        copy.wait_send()
    for copy in own:
        copy.wait()


def gather(members, planes, keys, values):
    kv_count, rows, depth = keys.shape
    out = pltpu.VMEM((members, rows, depth), keys.dtype)
    return pl.pallas_call(
        functools.partial(gather_kernel, members, planes, kv_count // planes),
        out_shape=(out, out),
        in_specs=[pl.BlockSpec(memory_space=pltpu.HBM)] * 2,
        out_specs=[pl.BlockSpec(memory_space=pltpu.VMEM)] * 2,
        scratch_shapes=[pltpu.SemaphoreType.DMA((2,))]
        + [pltpu.SemaphoreType.DMA((2, 2, members // 2))] * 6,
        compiler_params=pltpu.CompilerParams(
            collective_id=0, has_side_effects=True, vmem_limit_bytes=SMALL_VMEM_BYTES
        ),
        name="gather_keys",
    )(pltpu.with_memory_space_constraint(keys, pltpu.HBM), pltpu.with_memory_space_constraint(values, pltpu.HBM))


def dot(left, right):
    return jnp.dot(left, right, preferred_element_type=jnp.float32)


def dot_first(left, right):
    return lax.dot_general(left, right, (((0,), (0,)), ((), ())), preferred_element_type=jnp.float32)


def grad_kernel(members, order_ref, mask_ref, q_ref, g_ref, k_ref, v_ref, dq_ref, dkv_ref,
                list_ref, exp_ref, dprob_ref, top_ref, acc_ref, dq_acc, qt_ref, gt_ref):
    ctx = lax.axis_index("ctx")
    seq = ctx % SEQS
    member = ctx // SEQS
    depth = q_ref.shape[1]
    rows = q_ref.shape[0] // QB_DEV
    heads = rows // BLK
    slots = members * QB_DEV
    scale = depth ** -0.5
    scale2 = scale * math.log2(math.e)
    acc_ref[...] = jnp.zeros_like(acc_ref)
    query_pos = [order_ref[seq, member * QB_DEV + index] for index in range(QB_DEV)]

    def list_slot(slot, counts):
        key_pos = order_ref[seq, slot]
        grown = []
        for index, count in enumerate(counts):
            list_ref[index, count] = slot
            seen = jnp.logical_and(key_pos < query_pos[index], mask_ref[seq, query_pos[index], key_pos] == 1)
            grown.append(count + seen.astype(jnp.int32))
        return tuple(grown)

    counts = lax.fori_loop(0, slots, list_slot, (jnp.int32(0),) * QB_DEV, unroll=UNROLL)
    for index, count in enumerate(counts):
        list_ref[index, slots + 1] = count

    def blocks(ref, picked):
        return jnp.concatenate([ref[slot] for slot in picked], axis=0) if len(picked) > 1 else ref[picked[0]]

    def fold(value, op):
        return op(value.reshape(value.shape[0] // 8, 8, rows), axis=0)

    def spread(value, count):
        return jnp.broadcast_to(value[None], (count // 8, 8, rows)).reshape(count, rows)

    def query_block(index, carry):
        own = member * QB_DEV + index
        count = list_ref[index, slots + 1]
        at = pl.ds(pl.multiple_of(index * rows, rows), rows)
        qt_ref[...] = q_ref[at, :].T
        gt_ref[...] = g_ref[at, :].T

        def part(start, size, body, state):
            picked = [list_ref[index, start + offset] for offset in range(size)]
            where = pl.ds(pl.multiple_of((start + 1) * BLK, BLK), size * BLK)
            return body(picked, where, start + 1, state)

        def over(body, state):
            state = lax.fori_loop(0, count // WIDE, lambda n, state: part(n * WIDE, WIDE, body, state), state)
            size = WIDE // 2
            while size:
                start = count // (2 * size) * (2 * size)
                state = lax.cond(
                    count // size % 2 == 1,
                    lambda state, start=start, size=size: part(start, size, body, state),
                    lambda state: state,
                    state,
                )
                size //= 2
            return state

        def weigh(picked, where, number, state, diagonal=False):
            maxima, totals, weighted = state
            score = dot(blocks(k_ref, picked), qt_ref[...])
            if diagonal:
                key_token = lax.broadcasted_iota(jnp.int32, (BLK, rows), 0)
                query_token = lax.broadcasted_iota(jnp.int32, (BLK, rows), 1) // heads
                score = jnp.where(key_token <= query_token, score, NEG)
            dprob = dot(blocks(v_ref, picked), gt_ref[...])
            new = jnp.maximum(maxima, fold(score, jnp.max))
            top = new * scale2
            factor = jnp.exp2(maxima * scale2 - top)
            exp_part = jnp.exp2(score * scale2 - spread(top, score.shape[0]))
            exp_ref[where, :] = exp_part
            dprob_ref[where, :] = dprob
            top_ref[number] = top
            return (
                new,
                totals * factor + fold(exp_part, jnp.sum),
                weighted * factor + fold(exp_part * dprob, jnp.sum),
            )

        zero = jnp.zeros((8, rows), jnp.float32)
        first_at = pl.ds(0, BLK)
        state = weigh([own], first_at, 0, (zero + NEG, zero, zero), True)
        maxima, totals, weighted = over(weigh, state)
        tops = maxima * scale2
        top = jnp.broadcast_to(jnp.max(tops, axis=0, keepdims=True), (8, rows))
        factor = jnp.exp2(tops - top)
        inverse = 1.0 / jnp.sum(totals * factor, axis=0, keepdims=True)
        delta = jnp.broadcast_to(jnp.sum(weighted * factor, axis=0, keepdims=True) * inverse, (8, rows))
        inverse = jnp.broadcast_to(inverse, (8, rows))

        def grads(picked, where, number, state, first=False):
            size = len(picked) * BLK
            share = jnp.exp2(top_ref[number] - top) * inverse
            prob = exp_ref[where, :] * spread(share, size)
            dscore = (prob * (dprob_ref[where, :] - spread(delta, size))).astype(jnp.bfloat16)
            key_add = dot(dscore, q_ref[at, :])
            value_add = dot(prob.astype(jnp.bfloat16), g_ref[at, :])
            for offset, slot in enumerate(picked):
                acc_ref[0, slot] += key_add[offset * BLK:(offset + 1) * BLK]
                acc_ref[1, slot] += value_add[offset * BLK:(offset + 1) * BLK]
            add = dot_first(dscore, blocks(k_ref, picked))
            dq_acc[...] = add if first else dq_acc[...] + add
            return state

        grads([own], first_at, 0, 0, True)
        over(grads, 0)
        dq_ref[at, :] = (dq_acc[...] * scale).astype(dq_ref.dtype)
        return carry

    lax.fori_loop(0, QB_DEV, query_block, 0)
    dkv_ref[0] = (acc_ref[0] * scale).astype(dkv_ref.dtype)
    dkv_ref[1] = acc_ref[1].astype(dkv_ref.dtype)


def local_grads(members, block_pos, block_mask, query_rows, grad_rows, keys, values):
    row_total, depth = query_rows.shape
    slots = members * QB_DEV
    rows = row_total // QB_DEV
    smem = pl.BlockSpec(memory_space=pltpu.SMEM)
    vmem = pl.BlockSpec(memory_space=pltpu.VMEM)
    return pl.pallas_call(
        functools.partial(grad_kernel, members),
        out_shape=(
            jax.ShapeDtypeStruct((row_total, depth), jnp.bfloat16),
            pltpu.VMEM((2, slots, BLK, depth), jnp.bfloat16),
        ),
        in_specs=[smem, smem, vmem, vmem, vmem, vmem],
        out_specs=(vmem, vmem),
        scratch_shapes=[
            pltpu.SMEM((QB_DEV, slots + 2), jnp.int32),
            pltpu.VMEM((slots * BLK, rows), jnp.float32),
            pltpu.VMEM((slots * BLK, rows), jnp.float32),
            pltpu.VMEM((slots, 8, rows), jnp.float32),
            pltpu.VMEM((2, slots, BLK, depth), jnp.float32),
            pltpu.VMEM((rows, depth), jnp.float32),
            pltpu.VMEM((depth, rows), jnp.bfloat16),
            pltpu.VMEM((depth, rows), jnp.bfloat16),
        ],
        compiler_params=pltpu.CompilerParams(vmem_limit_bytes=VMEM_BYTES),
        name="local_grads",
    )(block_pos, block_mask, query_rows, grad_rows,
      keys.reshape(slots, BLK, depth), values.reshape(slots, BLK, depth))


def reduce_kernel(members, planes, part_ref, out_ref, side, give, given, sums, landed, piece,
                  side_send, side_recv, pair_send, pair_recv, ring_send, ring_recv, own_sem,
                  z_send, z_recv, x_send, x_recv, twin_send, twin_recv):
    place = Place(members, planes)
    half = part_ref.shape[2] // 2
    quarter = half // 2
    core = place.core
    keep = place.x % 2
    partner = place.head_id(place.z, place.x + 1 - 2 * keep, core)
    z_ids = [(place.z + step) % planes for step in range(1, planes)]
    x_ids = [(place.x + step) % X for step in range(1, X)]
    meet(
        [place.sibling()]
        + [place.along_y(steps) for steps in (1, -1, 2, -2)]
        + [place.head_id(place.z, x, core) for x in x_ids]
        + [place.head_id(z, place.x, core) for z in z_ids]
    )
    started = []

    def start(copy):
        copy.start()
        started.append(copy)

    offsets = [4, 3, -3, 1, -1, 2, -2, 0]

    def side_copy(steps):
        at = place.member(steps)
        slot = offsets.index(steps)
        return remote(part_ref.at[1 - core, at], side.at[slot], side_send.at[slot], side_recv.at[slot], place.sibling())

    def pair_copy(steps):
        slot = offsets.index(steps)
        return remote(give.at[slot], given.at[slot], pair_send.at[slot], pair_recv.at[slot], partner)

    def chip_sum(steps, which):
        rows_at = pl.ds(pl.multiple_of(which * half, half), half)
        return (part_ref[core, place.member(steps), rows_at, :].astype(jnp.float32)
                + side[offsets.index(steps), rows_at, :].astype(jnp.float32))

    def pair_sum(steps):
        pair_copy(steps).wait_recv()
        return chip_sum(steps, keep) + given[offsets.index(steps)].astype(jnp.float32)

    def ring_copy(way, reach, steps):
        rows_at = pl.ds(way * quarter, quarter) if reach == 4 else pl.ds(0, half)
        return remote(
            sums.at[way, reach - 1, rows_at],
            landed.at[way, reach - 1, rows_at],
            ring_send.at[way, reach - 1],
            ring_recv.at[way, reach - 1],
            place.along_y((1 - 2 * way) * steps),
        )

    def send(way, reach, steps, value):
        sums[way, reach - 1] = value.astype(sums.dtype)
        start(ring_copy(way, reach, steps))

    for steps in offsets:
        start(side_copy(steps))
    for steps in offsets:
        side_copy(steps).wait_recv()
        give[offsets.index(steps)] = chip_sum(steps, 1 - keep).astype(give.dtype)
        start(pair_copy(steps))
    far = pair_sum(4)
    for way in range(2):
        send(way, 4, 2, far)
    for reach in (3, 1):
        for way in range(2):
            send(way, reach, 1, pair_sum((1 - 2 * way) * reach))
    for way in range(2):
        value = pair_sum((1 - 2 * way) * 2)
        ring_copy(way, 3, 1).wait_recv()
        value = value + landed[way, 2].astype(jnp.float32)
        ring_copy(way, 4, 2).wait_recv()
        late = value[way * quarter:(way + 1) * quarter] + landed[
            way, 3, way * quarter:(way + 1) * quarter].astype(jnp.float32)
        early = value[(1 - way) * quarter:(2 - way) * quarter]
        send(way, 2, 2, jnp.concatenate([early, late] if way else [late, early], axis=0))
    value = pair_sum(0)
    for reach in (1, 2):
        for way in range(2):
            ring_copy(way, reach, 1).wait_recv()
            value = value + landed[way, reach - 1].astype(jnp.float32)
    piece[...] = value.astype(piece.dtype)

    def spot(tensor, z, x, sub=None):
        start_at, size = (0, half) if sub is None else (sub * quarter, quarter)
        rows_at = pl.ds(pl.multiple_of(x % 2 * half + start_at, size), size)
        return out_ref.at[tensor, z * (X // 2) + x // 2, rows_at]

    here = spot(core, place.z, place.x)
    for sub in range(2):
        for number, z in enumerate(z_ids):
            start(remote(piece.at[pl.ds(sub * quarter, quarter)], spot(core, place.z, place.x, sub),
                         z_send.at[number, sub], z_recv.at[number, sub], place.head_id(z, place.x, core)))
    for number, x in enumerate(x_ids):
        start(remote(piece, here, x_send.at[0, number, 0], x_recv.at[0, number, 0], place.head_id(place.z, x, core)))
    start(remote(piece, here, twin_send.at[0, 0], twin_recv.at[0, 0], place.sibling()))
    own = pltpu.make_async_copy(piece, here, own_sem)
    own.start()

    def landing(sem_send, sem_recv, spot_at):
        remote(spot_at, spot_at, sem_send, sem_recv, place.sibling()).wait_recv()

    def from_plane(number):
        return (place.z - number + planes) % planes

    def to_twin(number, index, x):
        spot_at = spot(core, from_plane(number), x)
        start(remote(spot_at, spot_at, twin_send.at[number, index], twin_recv.at[number, index], place.sibling()))

    for sub in range(2):
        for number in range(1, planes):
            spot_at = spot(core, from_plane(number), place.x, sub)
            landing(z_send.at[number - 1, sub], z_recv.at[number - 1, sub], spot_at)
            for index, x in enumerate(x_ids):
                start(remote(spot_at, spot_at, x_send.at[number, index, sub], x_recv.at[number, index, sub],
                             place.head_id(place.z, x, core)))
    for number in range(1, planes):
        to_twin(number, 0, place.x)
    for number in range(planes):
        for index in range(X - 1):
            x = (place.x - index - 1 + X) % X
            for sub in range(2) if number else (None,):
                landing(x_send.at[number, index, sub or 0], x_recv.at[number, index, sub or 0],
                        spot(core, from_plane(number), x, sub))
            to_twin(number, index + 1, x)
    for number in range(planes):
        for index in range(X):
            x = (place.x - index + X) % X
            landing(twin_send.at[number, index], twin_recv.at[number, index], spot(1 - core, from_plane(number), x))
    own.wait()
    for copy in started:
        copy.wait_send()


def reduce_sums(members, planes, kv_count, partial_sums):
    _, slots, _, depth = partial_sums.shape
    rows = slots // members * BLK
    half = rows // 2
    dma = pltpu.SemaphoreType.DMA
    low = jnp.bfloat16
    z_count = max(planes - 1, 1)
    return pl.pallas_call(
        functools.partial(reduce_kernel, members, planes),
        out_shape=pltpu.VMEM((2, kv_count, rows, depth), low),
        in_specs=[pl.BlockSpec(memory_space=pltpu.VMEM)],
        out_specs=pl.BlockSpec(memory_space=pltpu.VMEM),
        scratch_shapes=[
            pltpu.VMEM((members, rows, depth), low),
            pltpu.VMEM((members, half, depth), low),
            pltpu.VMEM((members, half, depth), low),
            pltpu.VMEM((2, 4, half, depth), low),
            pltpu.VMEM((2, 4, half, depth), low),
            pltpu.VMEM((half, depth), low),
            dma((members,)),
            dma((members,)),
            dma((members,)),
            dma((members,)),
            dma((2, 4)),
            dma((2, 4)),
            dma,
            dma((z_count, 2)),
            dma((z_count, 2)),
            dma((planes, X - 1, 2)),
            dma((planes, X - 1, 2)),
            dma((planes, X)),
            dma((planes, X)),
        ],
        compiler_params=pltpu.CompilerParams(
            collective_id=1, has_side_effects=True, vmem_limit_bytes=SMALL_VMEM_BYTES
        ),
        name="reduce_sums",
    )(partial_sums.reshape(2, members, rows, depth))


def per_device(queries, keys, values, d_out, block_pos, block_mask):
    members = lax.axis_size("ctx") // SEQS
    planes = lax.axis_size("head") // (CORES * X)
    tokens, heads, depth = queries.shape
    kv_count = keys.shape[1]
    key_all, value_all = gather(
        members, planes, jnp.transpose(keys, (1, 0, 2)), jnp.transpose(values, (1, 0, 2))
    )
    d_queries, partial_sums = local_grads(
        members,
        block_pos,
        block_mask,
        queries.reshape(tokens * heads, depth),
        d_out.reshape(tokens * heads, depth),
        key_all,
        value_all,
    )
    summed = reduce_sums(members, planes, kv_count, partial_sums)
    return (
        d_queries.reshape(tokens, heads, depth),
        jnp.transpose(summed[0], (1, 0, 2)),
        jnp.transpose(summed[1], (1, 0, 2)),
    )


def solution(mesh):
    placed = (
        P("ctx", "head", None),
        P("ctx", None, None),
        P("ctx", None, None),
        P("ctx", "head", None),
        P(),
        P(),
    )
    return jax.shard_map(
        per_device,
        mesh=mesh,
        in_specs=placed,
        out_specs=(P("ctx", "head", None), P("ctx", None, None), P("ctx", None, None)),
        check_vma=False,
    )
```

```python
import functools
import math

import jax
import jax.numpy as jnp
from jax import lax
from jax.experimental import pallas as pl
from jax.experimental.pallas import tpu as pltpu
from jax.sharding import PartitionSpec as P

GROUP = 16
BLK = 128
SEQS = 4
QB_DEV = 4
CORES = 2
X = 4
NEG = -1e30
WIDE = 8
UNROLL = 32
VMEM_BYTES = 44 * 1024 * 1024
SMALL_VMEM_BYTES = 16 * 1024 * 1024
MESH = pl.DeviceIdType.MESH


class Place:
    def __init__(self, members, planes):
        self.members = members
        self.planes = planes
        ctx = lax.axis_index("ctx")
        head = lax.axis_index("head")
        self.seq = ctx % SEQS
        self.y = ctx // SEQS
        self.core = head % CORES
        self.x = head // CORES % X
        self.z = head // (CORES * X)
        self.ctx = ctx
        self.head = head

    def member(self, steps):
        return (self.y + steps + self.members) % self.members

    def along_y(self, steps):
        return (self.member(steps) * SEQS + self.seq, self.head)

    def head_id(self, z, x, core):
        return (self.ctx, (z * X + x) * CORES + core)

    def sibling(self):
        return self.head_id(self.z, self.x, 1 - self.core)


def meet(partners):
    barrier = pltpu.get_barrier_semaphore()
    for partner in partners:
        pl.semaphore_signal(barrier, inc=1, device_id=partner, device_id_type=MESH)
    pl.semaphore_wait(barrier, len(partners))


def remote(src, dst, send_sem, recv_sem, target):
    return pltpu.make_async_remote_copy(
        src_ref=src,
        dst_ref=dst,
        send_sem=send_sem,
        recv_sem=recv_sem,
        device_id=target,
        device_id_type=MESH,
    )


def gather_kernel(members, planes, kv_per_plane, k_ref, v_ref, kg_ref, vg_ref, own_sem,
                  send_sem, recv_sem, pair_send, pair_recv, side_send, side_recv):
    place = Place(members, planes)
    part = k_ref.shape[1] // CORES
    quarter = part // 2
    kv = place.z * kv_per_plane + place.x * kv_per_plane // X
    lane = place.x % 2
    partner = place.head_id(place.z, place.x + 1 - 2 * lane, place.core)
    mine = pl.ds(pl.multiple_of(place.core * part, part), part)
    other = pl.ds(pl.multiple_of((1 - place.core) * part, part), part)
    kept = pl.ds(pl.multiple_of(place.core * part + lane * quarter, quarter), quarter)
    lacked = pl.ds(pl.multiple_of(place.core * part + (1 - lane) * quarter, quarter), quarter)
    pairs = ((k_ref, kg_ref), (v_ref, vg_ref))
    own = [
        pltpu.make_async_copy(src.at[kv], dst.at[place.y], own_sem.at[index])
        for index, (src, dst) in enumerate(pairs)
    ]
    meet([place.along_y(steps) for steps in (1, -1, 2, -2)] + [partner, place.sibling()])
    started = []
    chains = [(tensor, way) for tensor in range(2) for way in range(2)]

    def start(copy):
        copy.start()
        started.append(copy)

    def rows_of(reach):
        return mine if reach == 1 else kept

    def slab(tensor, way, reach, rows_at):
        return pairs[tensor][1].at[place.member(-(1 - 2 * way) * reach), rows_at]

    def send(tensor, way, origin, reach, steps):
        sign = 1 - 2 * way
        src_in, dst = pairs[tensor]
        at = dst.at[place.member(-sign * origin), rows_of(reach)]
        src = src_in.at[kv, rows_of(reach)] if origin == 0 else at
        start(remote(src, at, send_sem.at[tensor, way, reach - 1], recv_sem.at[tensor, way, reach - 1],
                     place.along_y(sign * steps)))

    def arrived(tensor, way, reach):
        at = slab(tensor, way, reach, rows_of(reach))
        remote(at, at, send_sem.at[tensor, way, reach - 1], recv_sem.at[tensor, way, reach - 1],
               place.sibling()).wait_recv()

    def pair_copy(tensor, way, reach, rows_at):
        at = slab(tensor, way, reach, rows_at)
        return remote(at, at, pair_send.at[tensor, way, reach - 1], pair_recv.at[tensor, way, reach - 1], partner)

    def side_copy(tensor, way, reach, rows_at):
        at = slab(tensor, way, reach, rows_at)
        return remote(at, at, side_send.at[tensor, way, reach - 1], side_recv.at[tensor, way, reach - 1],
                      place.sibling())

    for tensor, way in chains:
        send(tensor, way, 0, 2, 2)
    for tensor, way in chains:
        send(tensor, way, 0, 1, 1)
    for copy in own:
        copy.start()
    for tensor, way in chains:
        arrived(tensor, way, 2)
        if tensor == way:
            send(tensor, way, 2, 4, 2)
        send(tensor, way, 2, 3, 1)
        start(pair_copy(tensor, way, 2, kept))
    for tensor, way in chains:
        arrived(tensor, way, 1)
        start(side_copy(tensor, way, 1, mine))
    far = [(tensor, way, 3) for tensor, way in chains] + [(tensor, way, 4) for tensor, way in chains if tensor == way]
    for tensor, way, reach in far:
        arrived(tensor, way, reach)
        start(pair_copy(tensor, way, reach, kept))
    far = [(tensor, way, 2) for tensor, way in chains] + far
    for step in far:
        pair_copy(*step, lacked).wait_recv()
        start(side_copy(*step, mine))
    for step in [(tensor, way, 1) for tensor, way in chains] + far:
        side_copy(*step, other).wait_recv()
    for copy in started:
        copy.wait_send()
    for copy in own:
        copy.wait()


def gather(members, planes, keys, values):
    kv_count, rows, depth = keys.shape
    out = pltpu.VMEM((members, rows, depth), keys.dtype)
    return pl.pallas_call(
        functools.partial(gather_kernel, members, planes, kv_count // planes),
        out_shape=(out, out),
        in_specs=[pl.BlockSpec(memory_space=pltpu.HBM)] * 2,
        out_specs=[pl.BlockSpec(memory_space=pltpu.VMEM)] * 2,
        scratch_shapes=[pltpu.SemaphoreType.DMA((2,))]
        + [pltpu.SemaphoreType.DMA((2, 2, members // 2))] * 6,
        compiler_params=pltpu.CompilerParams(
            collective_id=0, has_side_effects=True, vmem_limit_bytes=SMALL_VMEM_BYTES
        ),
        name="gather_keys",
    )(pltpu.with_memory_space_constraint(keys, pltpu.HBM), pltpu.with_memory_space_constraint(values, pltpu.HBM))


def dot(left, right):
    return jnp.dot(left, right, preferred_element_type=jnp.float32)


def dot_first(left, right):
    return lax.dot_general(left, right, (((0,), (0,)), ((), ())), preferred_element_type=jnp.float32)


def grad_kernel(members, order_ref, mask_ref, q_ref, g_ref, k_ref, v_ref, dq_ref, dkv_ref,
                list_ref, exp_ref, dprob_ref, top_ref, acc_ref, dq_acc, qt_ref, gt_ref):
    ctx = lax.axis_index("ctx")
    seq = ctx % SEQS
    member = ctx // SEQS
    depth = q_ref.shape[1]
    rows = q_ref.shape[0] // QB_DEV
    heads = rows // BLK
    slots = members * QB_DEV
    scale = depth ** -0.5
    scale2 = scale * math.log2(math.e)
    acc_ref[...] = jnp.zeros_like(acc_ref)
    query_pos = [order_ref[seq, member * QB_DEV + index] for index in range(QB_DEV)]

    def list_slot(slot, counts):
        key_pos = order_ref[seq, slot]
        grown = []
        for index, count in enumerate(counts):
            list_ref[index, count] = slot
            seen = jnp.logical_and(key_pos < query_pos[index], mask_ref[seq, query_pos[index], key_pos] == 1)
            grown.append(count + seen.astype(jnp.int32))
        return tuple(grown)

    counts = lax.fori_loop(0, slots, list_slot, (jnp.int32(0),) * QB_DEV, unroll=UNROLL)
    for index, count in enumerate(counts):
        list_ref[index, slots + 1] = count

    def blocks(ref, picked):
        return jnp.concatenate([ref[slot] for slot in picked], axis=0) if len(picked) > 1 else ref[picked[0]]

    def fold(value, op):
        return op(value.reshape(value.shape[0] // 8, 8, rows), axis=0)

    def spread(value, count):
        return jnp.broadcast_to(value[None], (count // 8, 8, rows)).reshape(count, rows)

    def query_block(index, carry):
        own = member * QB_DEV + index
        count = list_ref[index, slots + 1]
        at = pl.ds(pl.multiple_of(index * rows, rows), rows)
        qt_ref[...] = q_ref[at, :].T
        gt_ref[...] = g_ref[at, :].T

        def part(start, size, body, state):
            picked = [list_ref[index, start + offset] for offset in range(size)]
            where = pl.ds(pl.multiple_of((start + 1) * BLK, BLK), size * BLK)
            return body(picked, where, start + 1, state)

        def over(body, state):
            state = lax.fori_loop(0, count // WIDE, lambda n, state: part(n * WIDE, WIDE, body, state), state)
            size = WIDE // 2
            while size:
                start = count // (2 * size) * (2 * size)
                state = lax.cond(
                    count // size % 2 == 1,
                    lambda state, start=start, size=size: part(start, size, body, state),
                    lambda state: state,
                    state,
                )
                size //= 2
            return state

        def weigh(picked, where, number, state, diagonal=False):
            maxima, totals, weighted = state
            score = dot(blocks(k_ref, picked), qt_ref[...])
            if diagonal:
                key_token = lax.broadcasted_iota(jnp.int32, (BLK, rows), 0)
                query_token = lax.broadcasted_iota(jnp.int32, (BLK, rows), 1) // heads
                score = jnp.where(key_token <= query_token, score, NEG)
            dprob = dot(blocks(v_ref, picked), gt_ref[...])
            new = jnp.maximum(maxima, fold(score, jnp.max))
            top = new * scale2
            factor = jnp.exp2(maxima * scale2 - top)
            exp_part = jnp.exp2(score * scale2 - spread(top, score.shape[0]))
            exp_ref[where, :] = exp_part
            dprob_ref[where, :] = dprob
            top_ref[number] = top
            return (
                new,
                totals * factor + fold(exp_part, jnp.sum),
                weighted * factor + fold(exp_part * dprob, jnp.sum),
            )

        zero = jnp.zeros((8, rows), jnp.float32)
        first_at = pl.ds(0, BLK)
        state = weigh([own], first_at, 0, (zero + NEG, zero, zero), True)
        maxima, totals, weighted = over(weigh, state)
        tops = maxima * scale2
        top = jnp.broadcast_to(jnp.max(tops, axis=0, keepdims=True), (8, rows))
        factor = jnp.exp2(tops - top)
        inverse = 1.0 / jnp.sum(totals * factor, axis=0, keepdims=True)
        delta = jnp.broadcast_to(jnp.sum(weighted * factor, axis=0, keepdims=True) * inverse, (8, rows))
        inverse = jnp.broadcast_to(inverse, (8, rows))

        def grads(picked, where, number, state, first=False):
            size = len(picked) * BLK
            share = jnp.exp2(top_ref[number] - top) * inverse
            prob = exp_ref[where, :] * spread(share, size)
            dscore = (prob * (dprob_ref[where, :] - spread(delta, size))).astype(jnp.bfloat16)
            key_add = dot(dscore, q_ref[at, :])
            value_add = dot(prob.astype(jnp.bfloat16), g_ref[at, :])
            for offset, slot in enumerate(picked):
                acc_ref[0, slot] += key_add[offset * BLK:(offset + 1) * BLK]
                acc_ref[1, slot] += value_add[offset * BLK:(offset + 1) * BLK]
            add = dot_first(dscore, blocks(k_ref, picked))
            dq_acc[...] = add if first else dq_acc[...] + add
            return state

        grads([own], first_at, 0, 0, True)
        over(grads, 0)
        dq_ref[at, :] = (dq_acc[...] * scale).astype(dq_ref.dtype)
        return carry

    lax.fori_loop(0, QB_DEV, query_block, 0)
    dkv_ref[0] = (acc_ref[0] * scale).astype(dkv_ref.dtype)
    dkv_ref[1] = acc_ref[1].astype(dkv_ref.dtype)


def local_grads(members, block_pos, block_mask, query_rows, grad_rows, keys, values):
    row_total, depth = query_rows.shape
    slots = members * QB_DEV
    rows = row_total // QB_DEV
    smem = pl.BlockSpec(memory_space=pltpu.SMEM)
    vmem = pl.BlockSpec(memory_space=pltpu.VMEM)
    return pl.pallas_call(
        functools.partial(grad_kernel, members),
        out_shape=(
            jax.ShapeDtypeStruct((row_total, depth), jnp.bfloat16),
            pltpu.VMEM((2, slots, BLK, depth), jnp.bfloat16),
        ),
        in_specs=[smem, smem, vmem, vmem, vmem, vmem],
        out_specs=(vmem, vmem),
        scratch_shapes=[
            pltpu.SMEM((QB_DEV, slots + 2), jnp.int32),
            pltpu.VMEM((slots * BLK, rows), jnp.float32),
            pltpu.VMEM((slots * BLK, rows), jnp.float32),
            pltpu.VMEM((slots, 8, rows), jnp.float32),
            pltpu.VMEM((2, slots, BLK, depth), jnp.float32),
            pltpu.VMEM((rows, depth), jnp.float32),
            pltpu.VMEM((depth, rows), jnp.bfloat16),
            pltpu.VMEM((depth, rows), jnp.bfloat16),
        ],
        compiler_params=pltpu.CompilerParams(vmem_limit_bytes=VMEM_BYTES),
        name="local_grads",
    )(block_pos, block_mask, query_rows, grad_rows,
      keys.reshape(slots, BLK, depth), values.reshape(slots, BLK, depth))


def reduce_kernel(members, planes, part_ref, out_ref, side, give, given, sums, landed, piece,
                  side_send, side_recv, pair_send, pair_recv, ring_send, ring_recv, own_sem,
                  z_send, z_recv, x_send, x_recv, twin_send, twin_recv):
    place = Place(members, planes)
    half = part_ref.shape[2] // 2
    quarter = half // 2
    core = place.core
    keep = place.x % 2
    partner = place.head_id(place.z, place.x + 1 - 2 * keep, core)
    z_ids = [(place.z + step) % planes for step in range(1, planes)]
    x_ids = [(place.x + step) % X for step in range(1, X)]
    meet(
        [place.sibling()]
        + [place.along_y(steps) for steps in (1, -1, 2, -2)]
        + [place.head_id(place.z, x, core) for x in x_ids]
        + [place.head_id(z, place.x, core) for z in z_ids]
    )
    started = []

    def start(copy):
        copy.start()
        started.append(copy)

    offsets = [4, 3, -3, 2, -2, 1, -1, 0]

    def side_copy(steps):
        at = place.member(steps)
        slot = offsets.index(steps)
        return remote(part_ref.at[1 - core, at], side.at[slot], side_send.at[slot], side_recv.at[slot], place.sibling())

    def pair_copy(steps):
        slot = offsets.index(steps)
        return remote(give.at[slot], given.at[slot], pair_send.at[slot], pair_recv.at[slot], partner)

    def chip_sum(steps, which):
        rows_at = pl.ds(pl.multiple_of(which * half, half), half)
        return (part_ref[core, place.member(steps), rows_at, :].astype(jnp.float32)
                + side[offsets.index(steps), rows_at, :].astype(jnp.float32))

    def pair_sum(steps):
        pair_copy(steps).wait_recv()
        return chip_sum(steps, keep) + given[offsets.index(steps)].astype(jnp.float32)

    def ring_copy(way, reach, steps):
        rows_at = pl.ds(way * quarter, quarter) if reach == 4 else pl.ds(0, half)
        return remote(
            sums.at[way, reach - 1, rows_at],
            landed.at[way, reach - 1, rows_at],
            ring_send.at[way, reach - 1],
            ring_recv.at[way, reach - 1],
            place.along_y((1 - 2 * way) * steps),
        )

    def send(way, reach, steps, value):
        sums[way, reach - 1] = value.astype(sums.dtype)
        start(ring_copy(way, reach, steps))

    for steps in offsets:
        start(side_copy(steps))
    for steps in offsets:
        side_copy(steps).wait_recv()
        give[offsets.index(steps)] = chip_sum(steps, 1 - keep).astype(give.dtype)
        start(pair_copy(steps))
    far = pair_sum(4)
    for way in range(2):
        send(way, 4, 2, far)
    for way in range(2):
        send(way, 3, 1, pair_sum((1 - 2 * way) * 3))
    for way in range(2):
        value = pair_sum((1 - 2 * way) * 2)
        ring_copy(way, 3, 1).wait_recv()
        value = value + landed[way, 2].astype(jnp.float32)
        ring_copy(way, 4, 2).wait_recv()
        late = value[way * quarter:(way + 1) * quarter] + landed[
            way, 3, way * quarter:(way + 1) * quarter].astype(jnp.float32)
        early = value[(1 - way) * quarter:(2 - way) * quarter]
        send(way, 2, 2, jnp.concatenate([early, late] if way else [late, early], axis=0))
    for way in range(2):
        send(way, 1, 1, pair_sum(1 - 2 * way))
    value = pair_sum(0)
    for reach in (1, 2):
        for way in range(2):
            ring_copy(way, reach, 1).wait_recv()
            value = value + landed[way, reach - 1].astype(jnp.float32)
    piece[...] = value.astype(piece.dtype)

    def spot(tensor, z, x, sub=None):
        start_at, size = (0, half) if sub is None else (sub * quarter, quarter)
        rows_at = pl.ds(pl.multiple_of(x % 2 * half + start_at, size), size)
        return out_ref.at[tensor, z * (X // 2) + x // 2, rows_at]

    here = spot(core, place.z, place.x)
    for sub in range(2):
        for number, z in enumerate(z_ids):
            start(remote(piece.at[pl.ds(sub * quarter, quarter)], spot(core, place.z, place.x, sub),
                         z_send.at[number, sub], z_recv.at[number, sub], place.head_id(z, place.x, core)))
    for number, x in enumerate(x_ids):
        start(remote(piece, here, x_send.at[0, number, 0], x_recv.at[0, number, 0], place.head_id(place.z, x, core)))
    start(remote(piece, here, twin_send.at[0, 0], twin_recv.at[0, 0], place.sibling()))
    own = pltpu.make_async_copy(piece, here, own_sem)
    own.start()

    def landing(sem_send, sem_recv, spot_at):
        remote(spot_at, spot_at, sem_send, sem_recv, place.sibling()).wait_recv()

    def from_plane(number):
        return (place.z - number + planes) % planes

    def to_twin(number, index, x):
        spot_at = spot(core, from_plane(number), x)
        start(remote(spot_at, spot_at, twin_send.at[number, index], twin_recv.at[number, index], place.sibling()))

    for sub in range(2):
        for number in range(1, planes):
            spot_at = spot(core, from_plane(number), place.x, sub)
            landing(z_send.at[number - 1, sub], z_recv.at[number - 1, sub], spot_at)
            for index, x in enumerate(x_ids):
                start(remote(spot_at, spot_at, x_send.at[number, index, sub], x_recv.at[number, index, sub],
                             place.head_id(place.z, x, core)))
    for number in range(1, planes):
        to_twin(number, 0, place.x)
    for number in range(planes):
        for index in range(X - 1):
            x = (place.x - index - 1 + X) % X
            for sub in range(2) if number else (None,):
                landing(x_send.at[number, index, sub or 0], x_recv.at[number, index, sub or 0],
                        spot(core, from_plane(number), x, sub))
            to_twin(number, index + 1, x)
    for number in range(planes):
        for index in range(X):
            x = (place.x - index + X) % X
            landing(twin_send.at[number, index], twin_recv.at[number, index], spot(1 - core, from_plane(number), x))
    own.wait()
    for copy in started:
        copy.wait_send()


def reduce_sums(members, planes, kv_count, partial_sums):
    _, slots, _, depth = partial_sums.shape
    rows = slots // members * BLK
    half = rows // 2
    dma = pltpu.SemaphoreType.DMA
    low = jnp.bfloat16
    z_count = max(planes - 1, 1)
    return pl.pallas_call(
        functools.partial(reduce_kernel, members, planes),
        out_shape=pltpu.VMEM((2, kv_count, rows, depth), low),
        in_specs=[pl.BlockSpec(memory_space=pltpu.VMEM)],
        out_specs=pl.BlockSpec(memory_space=pltpu.VMEM),
        scratch_shapes=[
            pltpu.VMEM((members, rows, depth), low),
            pltpu.VMEM((members, half, depth), low),
            pltpu.VMEM((members, half, depth), low),
            pltpu.VMEM((2, 4, half, depth), low),
            pltpu.VMEM((2, 4, half, depth), low),
            pltpu.VMEM((half, depth), low),
            dma((members,)),
            dma((members,)),
            dma((members,)),
            dma((members,)),
            dma((2, 4)),
            dma((2, 4)),
            dma,
            dma((z_count, 2)),
            dma((z_count, 2)),
            dma((planes, X - 1, 2)),
            dma((planes, X - 1, 2)),
            dma((planes, X)),
            dma((planes, X)),
        ],
        compiler_params=pltpu.CompilerParams(
            collective_id=1, has_side_effects=True, vmem_limit_bytes=SMALL_VMEM_BYTES
        ),
        name="reduce_sums",
    )(partial_sums.reshape(2, members, rows, depth))


def per_device(queries, keys, values, d_out, block_pos, block_mask):
    members = lax.axis_size("ctx") // SEQS
    planes = lax.axis_size("head") // (CORES * X)
    tokens, heads, depth = queries.shape
    kv_count = keys.shape[1]
    key_all, value_all = gather(
        members, planes, jnp.transpose(keys, (1, 0, 2)), jnp.transpose(values, (1, 0, 2))
    )
    d_queries, partial_sums = local_grads(
        members,
        block_pos,
        block_mask,
        queries.reshape(tokens * heads, depth),
        d_out.reshape(tokens * heads, depth),
        key_all,
        value_all,
    )
    summed = reduce_sums(members, planes, kv_count, partial_sums)
    return (
        d_queries.reshape(tokens, heads, depth),
        jnp.transpose(summed[0], (1, 0, 2)),
        jnp.transpose(summed[1], (1, 0, 2)),
    )


def solution(mesh):
    placed = (
        P("ctx", "head", None),
        P("ctx", None, None),
        P("ctx", None, None),
        P("ctx", "head", None),
        P(),
        P(),
    )
    return jax.shard_map(
        per_device,
        mesh=mesh,
        in_specs=placed,
        out_specs=(P("ctx", "head", None), P("ctx", None, None), P("ctx", None, None)),
        check_vma=False,
    )
```
